128 devices in a mesh: pipe: 8 (over z_lo, y), dp: 8 (over x, z_hi), tensor: 2 (over core).
Axes of the slice: x: 4, y: 4, z: 4 (z_hi: 2, z_lo: 2; z = z_hi * 2 + z_lo), core: 2. Of those that a mesh axis runs over, the one named last changes fastest.
Arguments:
- section_inputs: bfloat16 [8, 1024, 5120], P('pipe', 'dp'), may hold values from -6 to 6
- output_grad: bfloat16 [8, 1024, 5120], P('pipe', 'dp'), may hold values from -6 to 6
- norm_gain: float32 [8, 5120], P('pipe'), may hold values from 0.5 to 1.5
- weight: bfloat16 [8, 5120, 5120], P('pipe', 'tensor', 'dp'), may hold values from -0.078125 to 0.078125
- parked: bfloat16 [8, 3, 8, 16, 16, 5120], P('pipe', None, None, 'dp'), may hold values from -6 to 6
- in_flight: int32 [8], replicated, may hold values from 1 to 3
- old_hosts: int32 [8, 64, 1], P('pipe', 'dp'), may hold values from 0 to 7; in each aligned block of 8 rows (0 to 7, 8 to 15, ..., all dimensions but the last counted through in order) at most 2 rows name the same one
- new_hosts: int32 [8, 64, 1], P('pipe', 'dp'), may hold values from 0 to 7; in each aligned block of 8 rows (0 to 7, 8 to 15, ..., all dimensions but the last counted through in order) at most 2 rows name the same one
Outputs:
- section_output: bfloat16 [8, 1024, 5120], P('pipe', 'dp')
- input_grad: bfloat16 [8, 1024, 5120], P('pipe', 'dp')
- weight_grad: float32 [8, 5120, 5120], P('pipe', 'tensor', 'dp')
- gain_grad: float32 [8, 5120], P('pipe')
- parked_next: bfloat16 [8, 8, 16, 16, 5120], P('pipe', None, 'dp')
The draws below stay inside these ranges and needn't reach their ends.
Inputs may be any that keep to these rules, and one draw needn't show every extreme that they name: `old_hosts`: within the 8 blocks of one device no host section is named more than 2 times, and some host section is named exactly 2 times. `new_hosts`: within the 8 blocks of one device no host section is named more than 2 times, and some host section is named exactly 2 times.
All inputs are finite; a program needn't handle non-finite values.
Results may differ from the reference program's by a relative error of at most 0.0052.
Values may be sent and summed in bfloat16 or wider, within the bound.
A program may use at most 192 MiB of HBM per device.

```python
import math
import jax
import jax.numpy as jnp
import numpy as np
from jax import lax

D = 5120
NBLK = 8
CAP = 2
SLOTS = 3
BLOCK = 16
TOKENS = 1024
N_PIPE = 8
N_DP = 8


def set_ends(result, own_key, low, high):
    index_at = [jax.random.randint(jax.random.fold_in(own_key, axis), (), 0, length) for axis, length in enumerate(result.shape)]
    widest = result.shape.index(max(result.shape))
    next_to = index_at[:widest] + [(index_at[widest] + 1) % result.shape[widest]] + index_at[widest + 1:]
    return result.at[tuple(index_at)].set(low).at[tuple(next_to)].set(high)


def block_scale(own_key, shape, split, smallest, largest):
    level = 1.0
    for axis_at, shards_of in split:
        draws = jax.random.uniform(jax.random.fold_in(jax.random.fold_in(own_key, 6), axis_at), (shards_of,), jnp.float32, smallest / len(split), largest / len(split))
        level = level * jnp.repeat(jnp.exp(draws), shape[axis_at] // shards_of).reshape((-1,) + (1,) * (len(shape) - 1 - axis_at))
    return level


def assign_block(stream_key, own, number, rows, number_of, top, bound, lean):
    order = jax.random.permutation(stream_key, number_of)
    crowded, usual = shares(number_of, rows * top, bound, lean, True), shares(number_of, rows * top, bound, lean, False)
    places = jnp.arange(number_of)

    def named(lengths, turn):
        used = int((lengths > 0).sum())
        fixed = max(1, used // 4)
        shifted = fixed + (places - fixed + turn * (used - fixed)) % max(1, number_of - fixed)
        return jnp.zeros((number_of,), jnp.int32).at[order[jnp.where(places < fixed, places, shifted)]].set(jnp.asarray(lengths, jnp.int32))

    lengths = jnp.where(number % 4 == 0, named(crowded, number // 4), named(usual, number - number // 4 - 1))
    mixed = jax.random.permutation(jax.random.fold_in(own, 3), number_of)
    source_of, taker = mixed[0:number_of // 2 * 2:2], mixed[1:number_of // 2 * 2:2]
    margin = jnp.minimum(lengths[source_of] - 1, bound - lengths[taker]) // 2
    margin = jnp.where((source_of == order[0]) | (taker == order[0]) | (lengths[taker] == 0), 0, jnp.maximum(margin, 0))
    shifted = jax.random.randint(jax.random.fold_in(own, 4), (number_of // 2,), 0, 1 << 20) % (margin + 1)
    lengths = lengths.at[source_of].add(-shifted).at[taker].add(shifted)
    members = jnp.searchsorted(jnp.cumsum(lengths), jnp.arange(rows * top), side="right").astype(jnp.int32)
    listing = members.reshape(top, rows).T
    listing = listing[jax.random.permutation(jax.random.fold_in(own, 1), rows)]
    turn = jax.random.randint(jax.random.fold_in(own, 2), (rows, 1), 0, top)
    return jnp.take_along_axis(listing, (jnp.arange(top)[None, :] + turn) % top, axis=1)


def shares(count, total, limit, skew, full):
    loads = [(1 << 20) // math.isqrt(rank ** skew) + 1 for rank in range(1, count + 1)]
    largest = limit if full else min(limit, max(-(-total // count), total * loads[0] // sum(loads)))
    least = 1 if total - largest >= count - 1 else 0
    holding, rest = [largest] + [least] * (count - 1), total - largest - least * (count - 1)
    while rest > 0:
        movable = [i for i in range(1, count) if holding[i] < largest] or [i for i in range(1, count) if holding[i] < limit]
        pool, remaining = sum([loads[i] for i in movable]), rest
        for i in movable:
            addition = min(limit - holding[i], max(1, remaining * loads[i] // pool), rest)
            holding[i] = holding[i] + addition
            rest = rest - addition
    return np.array(holding)


def gaussian(stream_key, dims, scale, most, shards=(), kind=jnp.bfloat16):
    array = scale * jax.random.normal(stream_key, dims, jnp.float32)
    if shards:
        array = array * block_scale(stream_key, dims, shards, -0.22, 0.18)
    return jnp.clip(array, -most, most).astype(kind)


def setup_inputs(seed: int = 0) -> dict:
    arg_keys = jax.random.split(jax.random.key(seed), 9)
    section_inputs = gaussian(arg_keys[0], (N_PIPE, TOKENS, D), 1.0, 6.0, ((0, 8), (1, 8)))
    output_grad = gaussian(arg_keys[1], (N_PIPE, TOKENS, D), 1.0, 6.0, ((0, 8), (1, 8)))
    norm_gain = jnp.clip(1.0 + 0.1 * jax.random.normal(arg_keys[2], (N_PIPE, D), jnp.float32), 0.5, 1.5)
    weight = gaussian(arg_keys[3], (N_PIPE, D, D), D ** -0.5, 0.078125, ((0, 8), (1, 2), (2, 8)))
    parked = gaussian(arg_keys[4], (N_PIPE, SLOTS, N_PIPE, N_DP * CAP, BLOCK, D), 1.0, 6.0, ((0, 8), (3, 8)))
    in_flight = set_ends(jax.random.randint(arg_keys[5], (N_PIPE,), 1, SLOTS + 1), jax.random.fold_in(arg_keys[5], 1), 1, SLOTS).astype(jnp.int32)
    old_hosts_keys = jax.random.split(jax.random.fold_in(arg_keys[6], 1), N_PIPE * (N_DP * NBLK) // NBLK)
    old_hosts_turns = jax.random.permutation(jax.random.fold_in(arg_keys[6], 3), N_PIPE * (N_DP * NBLK) // NBLK)
    old_hosts = jax.vmap(lambda own, number: assign_block(jax.random.fold_in(arg_keys[6], 2), own, number, NBLK, N_PIPE, 1, CAP, 2))(old_hosts_keys, old_hosts_turns).reshape((N_PIPE, N_DP * NBLK, 1))
    new_hosts_keys = jax.random.split(jax.random.fold_in(arg_keys[7], 1), N_PIPE * (N_DP * NBLK) // NBLK)
    new_hosts_turns = jax.random.permutation(jax.random.fold_in(arg_keys[7], 3), N_PIPE * (N_DP * NBLK) // NBLK)
    new_hosts = jax.vmap(lambda own, number: assign_block(jax.random.fold_in(arg_keys[7], 2), own, number, NBLK, N_PIPE, 1, CAP, 2))(new_hosts_keys, new_hosts_turns).reshape((N_PIPE, N_DP * NBLK, 1))
    return dict(section_inputs=section_inputs, output_grad=output_grad, norm_gain=norm_gain, weight=weight, parked=parked, in_flight=in_flight, old_hosts=old_hosts, new_hosts=new_hosts)


eps = 1e-05

def apply_norm(rows):
    values = rows.astype(jnp.float32)
    scale = lax.rsqrt(lax.optimization_barrier(jnp.mean(values * values, axis=-1, keepdims=True)) + eps)
    return (values * scale, scale)

def block_ranks(routes):
    count = routes.shape[-1]
    same = routes[..., :, None] == routes[..., None, :]
    order = jnp.arange(count, dtype=jnp.int32)
    before = order[None, :] < order[:, None]
    return lax.optimization_barrier(jnp.sum(jnp.where(same & before, 1, 0), axis=-1)).astype(jnp.int32)

def reference(section_inputs, output_grad, norm_gain, weight, parked, in_flight, old_hosts, new_hosts):
    section_ids = jnp.arange(N_PIPE, dtype=jnp.int32)[:, None, None]
    group_ids = jnp.arange(N_DP, dtype=jnp.int32)[None, :, None]
    hosts_old = old_hosts[..., 0].reshape(N_PIPE, N_DP, NBLK).astype(jnp.int32)
    hosts_new = new_hosts[..., 0].reshape(N_PIPE, N_DP, NBLK).astype(jnp.int32)
    slot_ids = (in_flight - 1).astype(jnp.int32)[:, None, None]
    earlier = parked[hosts_old, slot_ids, section_ids, group_ids * CAP + block_ranks(hosts_old)]
    earlier = earlier.reshape(N_PIPE, TOKENS, D)
    pieces = section_inputs.reshape(N_PIPE, N_DP, NBLK, BLOCK, D)
    parked_next = jnp.zeros((N_PIPE, N_PIPE, N_DP * CAP, BLOCK, D), jnp.bfloat16)
    owner_ids = section_ids + jnp.zeros_like(hosts_new)
    parked_next = parked_next.at[hosts_new, owner_ids, group_ids * CAP + block_ranks(hosts_new)].set(pieces)
    outputs, input_grads, weight_grads, gain_grads = ([], [], [], [])
    for section_index in range(N_PIPE):
        scale_gain = norm_gain[section_index]
        centered_input, unused_value = apply_norm(section_inputs[section_index])
        norm_output = (centered_input * scale_gain).astype(jnp.bfloat16)
        update = jnp.dot(norm_output, weight[section_index], preferred_element_type=jnp.float32).astype(jnp.bfloat16)
        update = lax.optimization_barrier(update)
        outputs.append((section_inputs[section_index].astype(jnp.float32) + update.astype(jnp.float32)).astype(jnp.bfloat16))
        old_hat, old_scale = apply_norm(earlier[section_index])
        old_normed = (old_hat * scale_gain).astype(jnp.bfloat16)
        grads = output_grad[section_index]
        weight_grads.append(jnp.dot(old_normed.T, grads, preferred_element_type=jnp.float32))
        normed_grad = jnp.dot(grads, weight[section_index].T, preferred_element_type=jnp.float32)
        gain_grads.append(lax.optimization_barrier(jnp.sum(normed_grad * old_hat, axis=0)))
        scaled = normed_grad * scale_gain
        centred = scaled - old_hat * lax.optimization_barrier(jnp.mean(scaled * old_hat, axis=1, keepdims=True))
        input_grads.append((grads.astype(jnp.float32) + old_scale * centred).astype(jnp.bfloat16))
    return (jnp.stack(outputs), jnp.stack(input_grads), jnp.stack(weight_grads), jnp.stack(gain_grads), parked_next)
```

```python
import functools

import jax
import jax.numpy as jnp
from jax import lax
from jax.experimental import pallas as pl
from jax.experimental.pallas import tpu as pltpu
from jax.sharding import PartitionSpec as P

eps = 1e-05
MESH = pl.DeviceIdType.MESH
X = 4
CT = 512


def kernel(
    x_hbm, blocks_hbm, grad_hbm, gain_hbm, w_hbm, parked_hbm, flight, hosts_old, hosts_new,
    so_hbm, ig_hbm, wg_hbm, gg_hbm, pn_hbm,
    xf, xh, gh, gain, w, stage, p1s, p1r, early, oscale, p2s, gc,
    agx, ago, a2, b_r, b_l, rl2, rr2, rl1, rr1, zs, zr, ng,
    part, sib_part, up, ur, us, uin, so, ig, wg, gp, gsum,
    local_sem, a2a_s, a2a_r, p1_s, p1_r, p2_s, p2_r, agx_s, agx_r, ago_s, ago_r,
    rs_s, rs_r, sib_s, sib_r, up_s, up_r, gg_s, gg_r, out_sem,
):
    f32, bf16 = jnp.float32, jnp.bfloat16
    p = lax.axis_index("pipe")
    d = lax.axis_index("dp")
    c = lax.axis_index("tensor")
    xi, zh = d // 2, lax.rem(d, 2)
    o = 1 - c
    xr, xl, x2 = lax.rem(xi + 1, X), lax.rem(xi + 3, X), lax.rem(xi + 2, X)
    dz = xi * 2 + (1 - zh)
    dr, dl = xr * 2 + zh, xl * 2 + zh
    drz, dlz = xr * 2 + (1 - zh), xl * 2 + (1 - zh)
    hc = xh.shape[-1]
    oc = gc.shape[-1]
    right, left, zdev = (p, dr, c), (p, dl, c), (p, dz, c)
    sib = (p, d, o)
    half_c = pl.ds(pl.multiple_of(c * hc, 128), hc)

    def pipe_peer(k):
        return lax.rem(p + k, 8)

    def dp_peer(k):
        return lax.rem(d + k, 8)

    sends = []

    def remote(src, dst, ssem, rsem, dev):
        cp = pltpu.make_async_remote_copy(
            src_ref=src, dst_ref=dst, send_sem=ssem, recv_sem=rsem,
            device_id=dev, device_id_type=MESH,
        )
        cp.start()
        sends.append(cp)
        return cp

    def landed(dst, rsem):
        pltpu.make_async_copy(dst, dst, rsem).wait()

    def local(src, dst, sem):
        cp = pltpu.make_async_copy(src, dst, sem)
        cp.start()
        return cp

    c_xf = local(x_hbm, xf, local_sem.at[0])
    c_xh = local(blocks_hbm.at[:, :, half_c], xh.at[pl.ds(0, 8)], local_sem.at[1])
    c_gain = local(gain_hbm.at[:, half_c], gain, local_sem.at[2])
    c_stage = local(parked_hbm.at[:, :, :, :, half_c], stage, local_sem.at[3])
    c_w = local(w_hbm, w, local_sem.at[4])
    c_gh = local(grad_hbm.at[:, half_c], gh, local_sem.at[5])

    barrier = pltpu.get_barrier_semaphore()
    for k in range(1, 8):
        pl.semaphore_signal(barrier, inc=1, device_id=(pipe_peer(k), d, c), device_id_type=MESH)
        pl.semaphore_signal(barrier, inc=1, device_id=(p, dp_peer(k), c), device_id_type=MESH)
    pl.semaphore_signal(barrier, inc=1, device_id=sib, device_id_type=MESH)
    pl.semaphore_wait(barrier, 15)

    for k in (2, 6, 1, 3, 5, 7, 4):
        q = dp_peer(k)
        remote(
            grad_hbm.at[pl.ds(c * 64, 64), pl.ds(pl.multiple_of(q * oc, 128), oc)],
            gc.at[d, c], a2a_s.at[k], a2a_r.at[k], (p, q, c),
        )
    c_gown = local(
        grad_hbm.at[pl.ds(c * 64, 64), pl.ds(pl.multiple_of(d * oc, 128), oc)],
        gc.at[d, c], local_sem.at[6],
    )

    def gather_start(buf, ss, rs):
        remote(buf.at[d], buf.at[d], ss.at[0], rs.at[0], zdev)
        remote(buf.at[d], buf.at[d], ss.at[1], rs.at[1], right)
        remote(buf.at[d], buf.at[d], ss.at[3], rs.at[3], left)

    def gather_z(buf, ss, rs):
        landed(buf.at[dz], rs.at[0])
        remote(buf.at[dz], buf.at[dz], ss.at[2], rs.at[2], right)
        remote(buf.at[dz], buf.at[dz], ss.at[4], rs.at[4], left)

    def gather_forward(buf, ss, rs, at, from_left, from_right):
        landed(buf.at[from_left], rs.at[1 + at])
        remote(buf.at[from_left, 0], buf.at[from_left, 0], ss.at[5 + at], rs.at[5 + at], right)
        landed(buf.at[from_right], rs.at[3 + at])
        remote(buf.at[from_right, 1], buf.at[from_right, 1], ss.at[7 + at], rs.at[7 + at], left)

    def gather_end(buf, rs):
        for at in range(2):
            landed(buf.at[0, 0], rs.at[5 + at])
            landed(buf.at[0, 1], rs.at[7 + at])

    c_xf.wait()
    c_xh.wait()
    c_gain.wait()

    def norm_rows(i, _):
        rows = pl.ds(pl.multiple_of(i * 16, 16), 16)
        v = xf[rows, :].astype(f32)
        scale = lax.rsqrt(jnp.mean(v * v, axis=-1, keepdims=True) + eps)
        val = (xh[i].astype(f32) * scale * gain[...]).astype(bf16)
        agx[d, i // 4, pl.ds(pl.multiple_of(lax.rem(i, 4) * 16, 16), 16), :] = val
        return 0

    lax.fori_loop(0, 8, norm_rows, 0)
    gather_start(agx, agx_s, agx_r)

    c_stage.wait()

    def pick(s, _):
        p1s[s] = stage[jnp.maximum(flight[s] - 1, 0), s]
        return 0

    lax.fori_loop(0, 8, pick, 0)
    for k in range(1, 8):
        q = pipe_peer(k)
        remote(p1s.at[q], p1r.at[pl.ds(p * 2, 2)], p1_s.at[k], p1_r.at[k], (q, d, c))
    c_p1own = local(p1s.at[p], p1r.at[pl.ds(p * 2, 2)], local_sem.at[7])

    def place(hosts):
        h = [hosts[b] for b in range(8)]
        return [
            h[b] * 2 + sum([jnp.where(h[a] == h[b], 1, 0) for a in range(b)], jnp.int32(0))
            for b in range(8)
        ]

    xh[8] = jnp.zeros((16, hc), bf16)
    new_at = place(hosts_new)
    old_at = place(hosts_old)

    for slot in range(16):
        which = 8 + sum([jnp.where(new_at[b] == slot, b - 8, 0) for b in range(8)], jnp.int32(0))
        p2s[slot // 2, slot % 2] = xh[which]
    for k in range(1, 8):
        q = pipe_peer(k)
        remote(p2s.at[q], pn_hbm.at[p, :, :, half_c], p2_s.at[k], p2_r.at[k], (q, d, c))
    c_p2own = local(p2s.at[p], pn_hbm.at[p, :, :, half_c], local_sem.at[8])

    c_gown.wait()
    for k in range(1, 8):
        landed(gc.at[lax.rem(d + 8 - k, 8), c], a2a_r.at[k])
    remote(gc.at[:, c], gc.at[:, c], sib_s.at[0], sib_r.at[0], sib)
    c_w.wait()
    landed(gc.at[:, o], sib_r.at[0])

    def back(rows, t):
        return lax.dot_general(
            rows, w[pl.ds(pl.multiple_of(t * CT, CT), CT), :],
            (((1,), (1,)), ((), ())), preferred_element_type=f32,
        )

    def cols(t):
        return pl.ds(pl.multiple_of(t * CT, CT), CT)

    n_t = hc // CT

    def far(t, _):
        val = back(gc[pl.ds(x2 * 2, 2)].reshape(256, oc), t)
        a2[:, :, :, cols(t)] = val.astype(bf16).reshape(2, 2, 64, CT)
        return 0

    lax.fori_loop(0, n_t, far, 0)
    for j in range(2):
        remote(a2.at[j, 0], rl2.at[j], rs_s.at[j], rs_r.at[j], right)
        remote(a2.at[j, 1], rr2.at[j], rs_s.at[2 + j], rs_r.at[2 + j], left)

    def near(t, _):
        val = back(gc[pl.ds(xr * 2, 2), 1].reshape(128, oc), t)
        b_r[:, 1, :, cols(t)] = val.astype(bf16).reshape(2, 64, CT)
        val = back(gc[pl.ds(xl * 2, 2), 0].reshape(128, oc), t)
        b_l[:, 0, :, cols(t)] = val.astype(bf16).reshape(2, 64, CT)
        return 0

    lax.fori_loop(0, n_t, near, 0)
    for j in range(2):
        remote(b_r.at[j, 1], rl1.at[j, 1], rs_s.at[4 + j], rs_r.at[4 + j], right)
        remote(b_l.at[j, 0], rr1.at[j, 0], rs_s.at[6 + j], rs_r.at[6 + j], left)

    gather_z(agx, agx_s, agx_r)

    c_p1own.wait()
    for k in range(1, 8):
        landed(p1r.at[pl.ds(lax.rem(p + 8 - k, 8) * 2, 2)], p1_r.at[k])
    for b in range(8):
        early[pl.ds(b * 16, 16), :] = p1r[old_at[b]]

    def lanes(v):
        total = v[:, 0:128]
        for i in range(1, v.shape[1] // 128):
            total = total + v[:, i * 128:(i + 1) * 128]
        return total

    def squares(i, _):
        rows = pl.ds(pl.multiple_of(i * 16, 16), 16)
        v = early[rows, :].astype(f32)
        part[0, rows, :] = lanes(v * v)
        return 0

    lax.fori_loop(0, 8, squares, 0)
    remote(part.at[0], sib_part.at[0], sib_s.at[1], sib_r.at[1], sib)
    landed(sib_part.at[0], sib_r.at[1])

    def norm_old(i, _):
        rows = pl.ds(pl.multiple_of(i * 16, 16), 16)
        sq = jnp.sum(part[0, rows, :] + sib_part[0, rows, :], axis=-1, keepdims=True)
        scale = lax.rsqrt(sq / (2 * hc) + eps)
        oscale[rows, :] = jnp.broadcast_to(scale, (16, 128))
        val = (early[rows, :].astype(f32) * scale * gain[...]).astype(bf16)
        ago[d, i // 4, pl.ds(pl.multiple_of(lax.rem(i, 4) * 16, 16), 16), :] = val
        return 0

    lax.fori_loop(0, 8, norm_old, 0)
    gather_start(ago, ago_s, ago_r)

    gather_forward(agx, agx_s, agx_r, 0, dl, dr)

    for j in range(2):
        landed(rl2.at[j], rs_r.at[j])
        landed(rr2.at[j], rs_r.at[2 + j])

    def through(t, _):
        val = back(gc[pl.ds(xr * 2, 2), 0].reshape(128, oc), t)
        val = val + rl2[:, :, cols(t)].reshape(128, CT).astype(f32)
        b_r[:, 0, :, cols(t)] = val.astype(bf16).reshape(2, 64, CT)
        val = back(gc[pl.ds(xl * 2, 2), 1].reshape(128, oc), t)
        val = val + rr2[:, :, cols(t)].reshape(128, CT).astype(f32)
        b_l[:, 1, :, cols(t)] = val.astype(bf16).reshape(2, 64, CT)
        return 0

    lax.fori_loop(0, n_t, through, 0)
    for j in range(2):
        remote(b_r.at[j, 0], rl1.at[j, 0], rs_s.at[8 + j], rs_r.at[8 + j], right)
        remote(b_l.at[j, 1], rr1.at[j, 1], rs_s.at[10 + j], rs_r.at[10 + j], left)

    gather_forward(agx, agx_s, agx_r, 1, dlz, drz)
    gather_z(ago, ago_s, ago_r)

    c_p2own.wait()
    for k in range(1, 8):
        landed(pn_hbm.at[lax.rem(p + 8 - k, 8), :, :, half_c], p2_r.at[k])
    remote(pn_hbm.at[:, :, :, half_c], pn_hbm.at[:, :, :, half_c], sib_s.at[2], sib_r.at[2], sib)

    def project(xq, i):
        two = pl.ds(xq * 2, 2)

        def body(t, _):
            val = jnp.dot(
                agx[two, :, :, cols(t)].reshape(256, CT), w[cols(t), :],
                preferred_element_type=f32,
            ).reshape(2, 2, 64, oc)

            @pl.when(t == 0)
            def _():
                up[two] = val

            @pl.when(t > 0)
            def _():
                up[two] = up[two] + val

            return 0

        lax.fori_loop(0, n_t, body, 0)
        remote(up.at[two, o], ur.at[two], up_s.at[i], up_r.at[i], sib)

    def project_sum(xq, i):
        two = pl.ds(xq * 2, 2)
        landed(ur.at[two], up_r.at[i])
        us[two] = (up[two, c] + ur[two]).astype(bf16)

    project(xi, 0)
    project(xl, 1)
    project(xr, 2)
    gather_forward(ago, ago_s, ago_r, 0, dl, dr)
    project_sum(xi, 0)
    project_sum(xl, 1)
    project_sum(xr, 2)
    remote(us.at[dz], uin.at[d], up_s.at[4], up_r.at[4], zdev)
    remote(us.at[dl], uin.at[d], up_s.at[5], up_r.at[5], left)
    remote(us.at[dr], uin.at[d], up_s.at[6], up_r.at[6], right)
    remote(us.at[dlz], uin.at[d], up_s.at[7], up_r.at[7], (p, dlz, c))
    remote(us.at[drz], uin.at[d], up_s.at[8], up_r.at[8], (p, drz, c))

    for j in range(2):
        landed(rl1.at[j, 1], rs_r.at[4 + j])
        landed(rr1.at[j, 0], rs_r.at[6 + j])
        landed(rl1.at[j, 0], rs_r.at[8 + j])
        landed(rr1.at[j, 1], rs_r.at[10 + j])

    def to_z(t, _):
        val = back(gc[dz].reshape(128, oc), t)
        val = val + rl1[1 - zh, :, :, cols(t)].reshape(128, CT).astype(f32)
        val = val + rr1[1 - zh, :, :, cols(t)].reshape(128, CT).astype(f32)
        zs[:, cols(t)] = val.astype(bf16)
        return 0

    lax.fori_loop(0, n_t, to_z, 0)
    remote(zs, zr, rs_s.at[12], rs_r.at[12], zdev)

    gather_end(agx, agx_r)
    project(x2, 3)
    gather_forward(ago, ago_s, ago_r, 1, dlz, drz)
    project_sum(x2, 3)
    for z in range(2):
        remote(us.at[x2 * 2 + z], uin.at[d], up_s.at[9 + z], up_r.at[9 + lax.rem(z + zh, 2)], (p, x2 * 2 + z, c))

    def weight_part(xq, first):
        two = pl.ds(xq * 2, 2)

        def body(t, _):
            val = lax.dot_general(
                ago[two, :, :, cols(t)].reshape(256, CT), gc[two].reshape(256, oc),
                (((0,), (0,)), ((), ())), preferred_element_type=f32,
            )
            if first:
                wg[cols(t), :] = val
            else:
                wg[cols(t), :] = wg[cols(t), :] + val
            return 0

        lax.fori_loop(0, n_t, body, 0)

    weight_part(xi, True)
    weight_part(xl, False)
    weight_part(xr, False)

    landed(zr, rs_r.at[12])
    part[1] = jnp.zeros((128, 128), f32)

    def own(t, _):
        val = back(gc[d].reshape(128, oc), t)
        val = val + rl1[zh, :, :, cols(t)].reshape(128, CT).astype(f32)
        val = val + rr1[zh, :, :, cols(t)].reshape(128, CT).astype(f32)
        val = val + zr[:, cols(t)].astype(f32)
        ng[:, cols(t)] = val
        term = val * (early[:, cols(t)].astype(f32) * oscale[:, 0:1])
        gp[d, :, cols(t)] = jnp.sum(term, axis=0, keepdims=True)
        part[1] = part[1] + lanes(term * gain[:, cols(t)])
        return 0

    lax.fori_loop(0, n_t, own, 0)
    remote(part.at[1], sib_part.at[1], sib_s.at[3], sib_r.at[3], sib)
    for k in range(1, 8):
        q = dp_peer(k)
        remote(gp.at[d], gp.at[d], gg_s.at[k], gg_r.at[k], (p, q, c))

    uin[d] = us[d]
    landed(uin.at[0], up_r.at[4])
    landed(uin.at[0], up_r.at[5])
    landed(uin.at[0], up_r.at[6])
    landed(uin.at[0], up_r.at[7])
    landed(uin.at[0], up_r.at[8])
    landed(uin.at[0], up_r.at[9])
    landed(uin.at[0], up_r.at[10])
    mine = pl.ds(pl.multiple_of(c * 64, 64), 64)

    def add_update(q, _):
        at = pl.ds(pl.multiple_of(q * oc, 128), oc)
        so[:, at] = (xf[mine, at].astype(f32) + uin[q].astype(f32)).astype(bf16)
        return 0

    lax.fori_loop(0, 8, add_update, 0)
    c_so = local(so, so_hbm.at[mine, :], out_sem.at[0])
    remote(so, so_hbm.at[mine, :], sib_s.at[4], sib_r.at[4], sib)

    landed(sib_part.at[1], sib_r.at[3])
    c_gh.wait()

    def input_rows(i, _):
        rows = pl.ds(pl.multiple_of(i * 16, 16), 16)
        mean = jnp.sum(part[1, rows, :] + sib_part[1, rows, :], axis=-1, keepdims=True) / (2 * hc)
        scale = oscale[rows, 0:1]
        old_hat = early[rows, :].astype(f32) * scale
        centred = ng[rows, :] * gain[...] - old_hat * mean
        ig[rows, :] = (gh[rows, :].astype(f32) + scale * centred).astype(bf16)
        return 0

    lax.fori_loop(0, 8, input_rows, 0)
    c_ig = local(ig, ig_hbm.at[:, half_c], out_sem.at[1])
    remote(ig, ig_hbm.at[:, half_c], sib_s.at[5], sib_r.at[5], sib)

    for k in range(1, 8):
        landed(gp.at[0], gg_r.at[k])
    total = gp[0]
    for q in range(1, 8):
        total = total + gp[q]
    gsum[...] = total
    c_gg = local(gsum, gg_hbm.at[:, half_c], out_sem.at[2])
    remote(gsum, gg_hbm.at[:, half_c], sib_s.at[6], sib_r.at[6], sib)

    gather_end(ago, ago_r)
    c_wg = []
    two2 = pl.ds(x2 * 2, 2)
    for t in range(n_t):
        at = pl.ds(t * CT, CT)
        val = lax.dot_general(
            ago[two2, :, :, at].reshape(256, CT), gc[two2].reshape(256, oc),
            (((0,), (0,)), ((), ())), preferred_element_type=f32,
        )
        wg[at, :] = wg[at, :] + val
        c_wg.append(local(wg.at[at, :], wg_hbm.at[at, :], out_sem.at[3 + t]))

    half_o = pl.ds(pl.multiple_of(o * hc, 128), hc)
    landed(pn_hbm.at[:, :, :, half_o], sib_r.at[2])
    landed(so_hbm.at[pl.ds(pl.multiple_of(o * 64, 64), 64), :], sib_r.at[4])
    landed(ig_hbm.at[:, half_o], sib_r.at[5])
    landed(gg_hbm.at[:, half_o], sib_r.at[6])
    for cp in [c_so, c_ig, c_gg] + c_wg:
        cp.wait()
    for cp in sends:
        cp.wait_send()


def local(section_inputs, output_grad, norm_gain, weight, parked, in_flight, old_hosts, new_hosts):
    rows, width = section_inputs.shape[1:]
    hc, oc = weight.shape[1:]
    f32, bf16 = jnp.float32, jnp.bfloat16
    hbm = pl.BlockSpec(memory_space=pl.ANY)
    smem = pl.BlockSpec(memory_space=pltpu.SMEM)
    vm = pltpu.VMEM
    dma = pltpu.SemaphoreType.DMA
    outs = pl.pallas_call(
        kernel,
        out_shape=(
            jax.ShapeDtypeStruct((rows, width), bf16),
            jax.ShapeDtypeStruct((rows, width), bf16),
            jax.ShapeDtypeStruct((hc, oc), f32),
            jax.ShapeDtypeStruct((1, width), f32),
            jax.ShapeDtypeStruct((8, 2, 16, width), bf16),
        ),
        in_specs=[hbm] * 6 + [smem] * 3,
        out_specs=(hbm,) * 5,
        scratch_shapes=[
            vm((rows, width), bf16),
            vm((9, 16, hc), bf16),
            vm((rows, hc), bf16),
            vm((1, hc), f32),
            vm((hc, oc), bf16),
            vm((3, 8, 2, 16, hc), bf16),
            vm((8, 2, 16, hc), bf16),
            vm((16, 16, hc), bf16),
            vm((rows, hc), bf16),
            vm((rows, 128), f32),
            vm((8, 2, 16, hc), bf16),
            vm((8, 2, 64, oc), bf16),
            vm((8, 2, 64, hc), bf16),
            vm((8, 2, 64, hc), bf16),
            vm((2, 2, 64, hc), bf16),
            vm((2, 2, 64, hc), bf16),
            vm((2, 2, 64, hc), bf16),
            vm((2, 64, hc), bf16),
            vm((2, 64, hc), bf16),
            vm((2, 2, 64, hc), bf16),
            vm((2, 2, 64, hc), bf16),
            vm((rows, hc), bf16),
            vm((rows, hc), bf16),
            vm((rows, hc), f32),
            vm((2, rows, 128), f32),
            vm((2, rows, 128), f32),
            vm((8, 2, 64, oc), f32),
            vm((8, 64, oc), f32),
            vm((8, 64, oc), bf16),
            vm((8, 64, oc), bf16),
            vm((64, width), bf16),
            vm((rows, hc), bf16),
            vm((hc, oc), f32),
            vm((8, 1, hc), f32),
            vm((1, hc), f32),
            dma((9,)),
            dma((8,)), dma((8,)),
            dma((8,)), dma((8,)),
            dma((8,)), dma((8,)),
            dma((9,)), dma((9,)),
            dma((9,)), dma((9,)),
            dma((13,)), dma((13,)),
            dma((7,)), dma((7,)),
            dma((11,)), dma((11,)),
            dma((8,)), dma((8,)),
            dma((8,)),
        ],
        compiler_params=pltpu.CompilerParams(
            collective_id=0, has_side_effects=True, vmem_limit_bytes=62 * 2**20
        ),
        cost_estimate=pl.CostEstimate(flops=10 * 2**30, bytes_accessed=40 * 2**20, transcendentals=0),
        name="relay_step",
    )(
        section_inputs[0], section_inputs[0].reshape(8, 16, width), output_grad[0], norm_gain, weight[0], parked[0],
        in_flight, old_hosts[0, :, 0], new_hosts[0, :, 0],
    )
    so, ig, wg, gg, pn = outs
    return so[None], ig[None], wg[None], gg, pn[None]


def solution(mesh):
    in_specs = (
        P("pipe", "dp", None),
        P("pipe", "dp", None),
        P("pipe", None),
        P("pipe", "tensor", "dp"),
        P("pipe", None, None, "dp", None, None),
        P(),
        P("pipe", "dp", None),
        P("pipe", "dp", None),
    )
    out_specs = (
        P("pipe", "dp", None),
        P("pipe", "dp", None),
        P("pipe", "tensor", "dp"),
        P("pipe", None),
        P("pipe", None, "dp", None, None),
    )
    return jax.shard_map(local, mesh=mesh, in_specs=in_specs, out_specs=out_specs, check_vma=False)
```

```python
import functools

import jax
import jax.numpy as jnp
from jax import lax
from jax.experimental import pallas as pl
from jax.experimental.pallas import tpu as pltpu
from jax.sharding import PartitionSpec as P

eps = 1e-05
MESH = pl.DeviceIdType.MESH
X = 4
CT = 512


def kernel(
    x_hbm, blocks_hbm, grad_hbm, gain_hbm, w_hbm, parked_hbm, flight, hosts_old, hosts_new,
    so_hbm, ig_hbm, wg_hbm, gg_hbm, pn_hbm, ago2_hbm, gc2_hbm,
    xf, xh, gh, gain, w, stage, p1s, p1r, early, oscale, p2s, p2r, gc,
    agx, ago, a2, b_r, b_l, rz2, rl2, rr2, rl1, rr1, zs, zr, ng,
    part, sib_part, up, ur, us, uin, so, ig, wg, gp, gsum,
    local_sem, a2a_s, a2a_r, p1_s, p1_r, p2_s, p2_r, agx_s, agx_r, ago_s, ago_r,
    rs_s, rs_r, sib_s, sib_r, up_s, up_r, gg_s, gg_r, out_sem,
):
    f32, bf16 = jnp.float32, jnp.bfloat16
    p = lax.axis_index("pipe")
    d = lax.axis_index("dp")
    c = lax.axis_index("tensor")
    xi, zh = d // 2, lax.rem(d, 2)
    o = 1 - c
    xr, xl, x2 = lax.rem(xi + 1, X), lax.rem(xi + 3, X), lax.rem(xi + 2, X)
    dz = xi * 2 + (1 - zh)
    dr, dl = xr * 2 + zh, xl * 2 + zh
    dx2, dx2z = x2 * 2 + zh, x2 * 2 + (1 - zh)
    drz, dlz = xr * 2 + (1 - zh), xl * 2 + (1 - zh)
    hc = xh.shape[-1]
    oc = gc.shape[-1]
    right, left, zdev = (p, dr, c), (p, dl, c), (p, dz, c)
    sib = (p, d, o)
    half_c = pl.ds(pl.multiple_of(c * hc, 128), hc)

    def pipe_peer(k):
        return lax.rem(p + k, 8)

    def dp_peer(k):
        return lax.rem(d + k, 8)

    sends = []

    def remote(src, dst, ssem, rsem, dev):
        cp = pltpu.make_async_remote_copy(
            src_ref=src, dst_ref=dst, send_sem=ssem, recv_sem=rsem,
            device_id=dev, device_id_type=MESH,
        )
        cp.start()
        sends.append(cp)
        return cp

    def landed(dst, rsem):
        pltpu.make_async_copy(dst, dst, rsem).wait()

    def local(src, dst, sem):
        cp = pltpu.make_async_copy(src, dst, sem)
        cp.start()
        return cp

    c_gown = local(
        grad_hbm.at[pl.ds(c * 64, 64), pl.ds(pl.multiple_of(d * oc, 128), oc)],
        gc.at[d, c], local_sem.at[6],
    )
    c_xf = local(x_hbm, xf, local_sem.at[0])
    c_xh = local(blocks_hbm.at[:, :, half_c], xh.at[pl.ds(0, 8)], local_sem.at[1])
    c_gain = local(gain_hbm.at[:, half_c], gain, local_sem.at[2])
    c_stage = local(parked_hbm.at[:, :, :, :, half_c], stage, local_sem.at[3])
    c_w = local(w_hbm, w, local_sem.at[4])
    c_gh = local(grad_hbm.at[:, half_c], gh, local_sem.at[5])
    later = []

    barrier = pltpu.get_barrier_semaphore()
    for k in range(1, 8):
        pl.semaphore_signal(barrier, inc=1, device_id=(pipe_peer(k), d, c), device_id_type=MESH)
        pl.semaphore_signal(barrier, inc=1, device_id=(p, dp_peer(k), c), device_id_type=MESH)
    pl.semaphore_signal(barrier, inc=1, device_id=sib, device_id_type=MESH)
    pl.semaphore_wait(barrier, 15)

    def cols(t):
        return pl.ds(pl.multiple_of(t * CT, CT), CT)

    n_t = hc // CT

    def loop(n):
        def run(body):
            def step(i, _):
                body(i)
                return 0

            lax.fori_loop(0, n, step, 0)

        return run

    def back(rows, t):
        return lax.dot_general(
            rows, w[cols(t), :], (((1,), (1,)), ((), ())), preferred_element_type=f32
        )

    def lanes(v):
        total = v[:, 0:128]
        for i in range(1, v.shape[1] // 128):
            total = total + v[:, i * 128:(i + 1) * 128]
        return total

    def place(hosts):
        h = [hosts[b] for b in range(8)]
        return [
            h[b] * 2 + sum([jnp.where(h[a] == h[b], 1, 0) for a in range(b)], jnp.int32(0))
            for b in range(8)
        ]

    def grads_out():
        for k in (2, 6, 1, 3, 5, 7, 4):
            q = dp_peer(k)
            remote(
                grad_hbm.at[pl.ds(c * 64, 64), pl.ds(pl.multiple_of(q * oc, 128), oc)],
                gc.at[d, c], a2a_s.at[k], a2a_r.at[k], (p, q, c),
            )

    def grads_sib():
        c_gown.wait()
        for k in range(1, 8):
            landed(gc.at[lax.rem(d + 8 - k, 8), c], a2a_r.at[k])
        remote(gc.at[:, c], gc.at[:, c], sib_s.at[0], sib_r.at[0], sib)

    def grads_in():
        c_w.wait()
        landed(gc.at[:, o], sib_r.at[0])

    def norm_new():
        c_xf.wait()
        c_xh.wait()
        c_gain.wait()

        @loop(8)
        def _(i):
            rows = pl.ds(pl.multiple_of(i * 16, 16), 16)
            v = xf[rows, :].astype(f32)
            scale = lax.rsqrt(jnp.mean(v * v, axis=-1, keepdims=True) + eps)
            val = (xh[i].astype(f32) * scale * gain[...]).astype(bf16)
            agx[d, i // 4, pl.ds(pl.multiple_of(lax.rem(i, 4) * 16, 16), 16), :] = val

    def own_z(buf, ss, rs):
        remote(buf.at[d], buf.at[d], ss.at[0], rs.at[0], zdev)

    def own_x(buf, ss, rs):
        remote(buf.at[d], buf.at[d], ss.at[1], rs.at[1], right)
        remote(buf.at[d], buf.at[d], ss.at[3], rs.at[3], left)

    def z_x(buf, ss, rs):
        landed(buf.at[dz], rs.at[0])
        remote(buf.at[dz], buf.at[dz], ss.at[2], rs.at[2], right)
        remote(buf.at[dz], buf.at[dz], ss.at[4], rs.at[4], left)

    def far_x(buf, ss, rs):
        landed(buf.at[dl], rs.at[1])
        remote(buf.at[dl, 0], buf.at[dl, 0], ss.at[5], rs.at[5], right)
        landed(buf.at[dr], rs.at[3])
        remote(buf.at[dr, 1], buf.at[dr, 1], ss.at[7], rs.at[7], left)

    def near_z(buf, rs):
        landed(buf.at[dlz], rs.at[2])
        landed(buf.at[drz], rs.at[4])

    def new_z():
        own_z(agx, agx_s, agx_r)

    def new_x():
        own_x(agx, agx_s, agx_r)

    def new_zx():
        z_x(agx, agx_s, agx_r)

    def new_far():
        far_x(agx, agx_s, agx_r)

    def new_far_z():
        landed(agx.at[dx2, 0], agx_r.at[5])
        remote(agx.at[dx2, 0], agx.at[dx2, 0], agx_s.at[6], agx_r.at[6], zdev)
        landed(agx.at[dx2, 1], agx_r.at[7])
        remote(agx.at[dx2, 1], agx.at[dx2, 1], agx_s.at[8], agx_r.at[8], zdev)

    def new_near():
        near_z(agx, agx_r)

    def stash_out():
        c_stage.wait()

        @loop(8)
        def _(s):
            p1s[s] = stage[jnp.maximum(flight[s] - 1, 0), s]

        for k in range(1, 8):
            q = pipe_peer(k)
            remote(p1s.at[q], p1r.at[pl.ds(p * 2, 2)], p1_s.at[k], p1_r.at[k], (q, d, c))
        later.append(local(p1s.at[p], p1r.at[pl.ds(p * 2, 2)], local_sem.at[7]))

    def norm_old():
        later.pop(0).wait()
        for k in range(1, 8):
            landed(p1r.at[pl.ds(lax.rem(p + 8 - k, 8) * 2, 2)], p1_r.at[k])
        old_at = place(hosts_old)
        for b in range(8):
            v = p1r[old_at[b]]
            early[pl.ds(b * 16, 16), :] = v
            v = v.astype(f32)
            part[0, pl.ds(b * 16, 16), :] = lanes(v * v)
        remote(part.at[0], sib_part.at[0], sib_s.at[1], sib_r.at[1], sib)
        landed(sib_part.at[0], sib_r.at[1])

        @loop(8)
        def _(i):
            rows = pl.ds(pl.multiple_of(i * 16, 16), 16)
            sq = jnp.sum(part[0, rows, :] + sib_part[0, rows, :], axis=-1, keepdims=True)
            scale = lax.rsqrt(sq / (2 * hc) + eps)
            oscale[rows, :] = jnp.broadcast_to(scale, (16, 128))
            val = (early[rows, :].astype(f32) * scale * gain[...]).astype(bf16)
            ago[d, i // 4, pl.ds(pl.multiple_of(lax.rem(i, 4) * 16, 16), 16), :] = val

    def old_z():
        own_z(ago, ago_s, ago_r)

    def old_x():
        own_x(ago, ago_s, ago_r)

    def old_zx():
        z_x(ago, ago_s, ago_r)

    def old_far():
        far_x(ago, ago_s, ago_r)

    def old_far_z():
        for h, n in ((0, 5), (1, 7)):
            landed(ago.at[dx2, h], ago_r.at[n])
            remote(
                ago.at[dx2, h, pl.ds(32, 32)], ago.at[dx2, h, pl.ds(32, 32)],
                ago_s.at[n + 4], ago_r.at[n + 4], zdev,
            )

    def old_far_x():
        near_z(ago, ago_r)
        for h, n, at, to in ((0, 6, dlz, right), (1, 8, drz, left)):
            remote(
                ago.at[at, h, pl.ds(0, 32)], ago.at[at, h, pl.ds(0, 32)],
                ago_s.at[n], ago_r.at[n], to,
            )

    def park_out():
        xh[8] = jnp.zeros((16, hc), bf16)
        new_at = place(hosts_new)
        for slot in range(16):
            which = 8 + sum([jnp.where(new_at[b] == slot, b - 8, 0) for b in range(8)], jnp.int32(0))
            p2s[slot // 2, slot % 2] = xh[which]
        for k in range(1, 8):
            q = pipe_peer(k)
            remote(p2s.at[q], p2r.at[p], p2_s.at[k], p2_r.at[k], (q, d, c))
        later.append(local(p2s.at[p], p2r.at[p], local_sem.at[8]))

    def park_sib():
        later.pop(0).wait()
        for k in range(1, 8):
            landed(p2r.at[lax.rem(p + 8 - k, 8)], p2_r.at[k])
        ends.append(local(p2r, pn_hbm.at[:, :, :, half_c], out_sem.at[6]))
        remote(p2r, pn_hbm.at[:, :, :, half_c], sib_s.at[2], sib_r.at[2], sib)

    def sum_far_z():
        @loop(n_t)
        def _(t):
            val = back(gc[dx2z].reshape(128, oc), t)
            a2[1, :, :, cols(t)] = val.astype(bf16).reshape(2, 64, CT)

        remote(a2.at[1], rz2, rs_s.at[0], rs_r.at[0], zdev)

    def sum_near_z():
        @loop(n_t)
        def _(t):
            val = back(gc[drz].reshape(128, oc), t)
            b_r[1 - zh, :, :, cols(t)] = val.astype(bf16).reshape(2, 64, CT)
            val = back(gc[dlz].reshape(128, oc), t)
            b_l[1 - zh, :, :, cols(t)] = val.astype(bf16).reshape(2, 64, CT)

        remote(b_r.at[1 - zh], rl1.at[1 - zh], rs_s.at[3], rs_r.at[3], right)
        remote(b_l.at[1 - zh], rr1.at[1 - zh], rs_s.at[4], rs_r.at[4], left)

    def sum_near():
        @loop(n_t)
        def _(t):
            b_r[zh, 1, :, cols(t)] = back(gc[dr, 1], t).astype(bf16)
            b_l[zh, 0, :, cols(t)] = back(gc[dl, 0], t).astype(bf16)

        remote(b_r.at[zh, 1], rl1.at[zh, 1], rs_s.at[5], rs_r.at[5], right)
        remote(b_l.at[zh, 0], rr1.at[zh, 0], rs_s.at[6], rs_r.at[6], left)

    def sum_far():
        landed(rz2, rs_r.at[0])

        @loop(n_t)
        def _(t):
            val = back(gc[dx2].reshape(128, oc), t)
            val = val + rz2[:, :, cols(t)].reshape(128, CT).astype(f32)
            a2[0, :, :, cols(t)] = val.astype(bf16).reshape(2, 64, CT)

        remote(a2.at[0, 0], rl2, rs_s.at[1], rs_r.at[1], right)
        remote(a2.at[0, 1], rr2, rs_s.at[2], rs_r.at[2], left)

    def sum_through():
        landed(rl2, rs_r.at[1])
        landed(rr2, rs_r.at[2])

        @loop(n_t)
        def _(t):
            val = back(gc[dr, 0], t) + rl2[:, cols(t)].astype(f32)
            b_r[zh, 0, :, cols(t)] = val.astype(bf16)
            val = back(gc[dl, 1], t) + rr2[:, cols(t)].astype(f32)
            b_l[zh, 1, :, cols(t)] = val.astype(bf16)

        remote(b_r.at[zh, 0], rl1.at[zh, 0], rs_s.at[7], rs_r.at[7], right)
        remote(b_l.at[zh, 1], rr1.at[zh, 1], rs_s.at[8], rs_r.at[8], left)

    def sum_z():
        landed(rl1.at[1 - zh], rs_r.at[3])
        landed(rr1.at[1 - zh], rs_r.at[4])

        @loop(n_t)
        def _(t):
            val = back(gc[dz].reshape(128, oc), t)
            val = val + rl1[1 - zh, :, :, cols(t)].reshape(128, CT).astype(f32)
            val = val + rr1[1 - zh, :, :, cols(t)].reshape(128, CT).astype(f32)
            zs[:, cols(t)] = val.astype(bf16)

        remote(zs, zr, rs_s.at[9], rs_r.at[9], zdev)

    def sum_own():
        landed(rl1.at[zh, 1], rs_r.at[5])
        landed(rr1.at[zh, 0], rs_r.at[6])
        landed(rl1.at[zh, 0], rs_r.at[7])
        landed(rr1.at[zh, 1], rs_r.at[8])
        landed(zr, rs_r.at[9])
        part[1] = jnp.zeros((128, 128), f32)

        @loop(n_t)
        def _(t):
            val = back(gc[d].reshape(128, oc), t)
            val = val + rl1[zh, :, :, cols(t)].reshape(128, CT).astype(f32)
            val = val + rr1[zh, :, :, cols(t)].reshape(128, CT).astype(f32)
            val = val + zr[:, cols(t)].astype(f32)
            ng[:, cols(t)] = val
            term = val * (early[:, cols(t)].astype(f32) * oscale[:, 0:1])
            gp[d, :, cols(t)] = jnp.sum(term, axis=0, keepdims=True)
            part[1] = part[1] + lanes(term * gain[:, cols(t)])

        remote(part.at[1], sib_part.at[1], sib_s.at[3], sib_r.at[3], sib)
        for k in range(1, 8):
            remote(gp.at[d], gp.at[d], gg_s.at[k], gg_r.at[k], (p, dp_peer(k), c))

    def project(xq, i):
        two = pl.ds(xq * 2, 2)

        @loop(n_t)
        def _(t):
            val = jnp.dot(
                agx[two, :, :, cols(t)].reshape(256, CT), w[cols(t), :],
                preferred_element_type=f32,
            ).reshape(2, 2, 64, oc)

            @pl.when(t == 0)
            def _():
                up[two] = val

            @pl.when(t > 0)
            def _():
                up[two] = up[two] + val

        remote(up.at[two, o], ur.at[two], up_s.at[i], up_r.at[i], sib)

    def project_sum(xq, i):
        two = pl.ds(xq * 2, 2)
        landed(ur.at[two], up_r.at[i])
        us[two] = (up[two, c] + ur[two]).astype(bf16)

    def project_near():
        project(xi, 0)
        project(xl, 1)
        project(xr, 2)

    def update_near():
        project_sum(xi, 0)
        project_sum(xl, 1)
        project_sum(xr, 2)
        uin[d] = us[d]
        remote(us.at[dz], uin.at[d], up_s.at[4], up_r.at[4], zdev)
        remote(us.at[dl], uin.at[d], up_s.at[5], up_r.at[5], left)
        remote(us.at[dr], uin.at[d], up_s.at[6], up_r.at[6], right)
        remote(us.at[dlz], uin.at[d], up_s.at[7], up_r.at[7], (p, dlz, c))
        remote(us.at[drz], uin.at[d], up_s.at[8], up_r.at[8], (p, drz, c))

    def update_far():
        landed(agx.at[dx2z, 0], agx_r.at[6])
        landed(agx.at[dx2z, 1], agx_r.at[8])
        project(x2, 3)
        project_sum(x2, 3)
        remote(us.at[dx2], uin.at[d], up_s.at[9], up_r.at[9], (p, dx2, c))
        remote(us.at[dx2z], uin.at[d], up_s.at[10], up_r.at[10], (p, dx2z, c))

    mine = pl.ds(pl.multiple_of(c * 64, 64), 64)

    def output():
        for k, at in ((4, dz), (5, dr), (6, dl), (7, drz), (8, dlz), (9, dx2), (10, dx2z)):
            landed(uin.at[at], up_r.at[k])

        @loop(8)
        def _(q):
            at = pl.ds(pl.multiple_of(q * oc, 128), oc)
            so[:, at] = (xf[mine, at].astype(f32) + uin[q].astype(f32)).astype(bf16)

        ends.append(local(so, so_hbm.at[mine, :], out_sem.at[0]))
        remote(so, so_hbm.at[mine, :], sib_s.at[4], sib_r.at[4], sib)

    def input_out():
        landed(sib_part.at[1], sib_r.at[3])
        c_gh.wait()

        @loop(8)
        def _(i):
            rows = pl.ds(pl.multiple_of(i * 16, 16), 16)
            mean = jnp.sum(part[1, rows, :] + sib_part[1, rows, :], axis=-1, keepdims=True) / (2 * hc)
            scale = oscale[rows, 0:1]
            old_hat = early[rows, :].astype(f32) * scale
            centred = ng[rows, :] * gain[...] - old_hat * mean
            ig[rows, :] = (gh[rows, :].astype(f32) + scale * centred).astype(bf16)

        ends.append(local(ig, ig_hbm.at[:, half_c], out_sem.at[1]))
        remote(ig, ig_hbm.at[:, half_c], sib_s.at[5], sib_r.at[5], sib)

    def gain_out():
        for k in range(1, 8):
            landed(gp.at[0], gg_r.at[k])
        total = gp[0]
        for q in range(1, 8):
            total = total + gp[q]
        gsum[...] = total
        ends.append(local(gsum, gg_hbm.at[:, half_c], out_sem.at[2]))
        remote(gsum, gg_hbm.at[:, half_c], sib_s.at[6], sib_r.at[6], sib)

    def weight_part(xq, first):
        two = pl.ds(xq * 2, 2)

        @loop(n_t)
        def _(t):
            val = lax.dot_general(
                ago[two, :, :, cols(t)].reshape(256, CT), gc[two].reshape(256, oc),
                (((0,), (0,)), ((), ())), preferred_element_type=f32,
            )
            if first:
                wg[cols(t), :] = val
            else:
                wg[cols(t), :] = wg[cols(t), :] + val

    def weight_own():
        weight_part(xi, True)

    def weight_near():
        weight_part(xl, False)
        weight_part(xr, False)
        ends.append(local(wg, wg_hbm, out_sem.at[3]))
        ends.append(local(gc.at[pl.ds(x2 * 2, 2)], gc2_hbm, out_sem.at[4]))

    def weight_rows():
        for n in (6, 8, 9, 11):
            landed(ago.at[dx2z, 0, pl.ds(0, 32)], ago_r.at[n])
        ends.append(local(ago.at[pl.ds(x2 * 2, 2)], ago2_hbm, out_sem.at[5]))

    ends = []
    for step in (
        grads_out, norm_new, stash_out, new_x, grads_sib, new_z, grads_in, sum_far_z,
        sum_near_z, new_far, sum_near, new_zx, new_far_z, park_out, sum_far, norm_old,
        sum_through, new_near, old_x, old_z, project_near, park_sib, update_far, old_far,
        old_zx, weight_own, sum_z, update_near, sum_own, old_far_z, input_out, output,
        old_far_x, weight_near, gain_out, weight_rows,
    ):
        step()

    half_o = pl.ds(pl.multiple_of(o * hc, 128), hc)
    landed(pn_hbm.at[:, :, :, half_o], sib_r.at[2])
    landed(so_hbm.at[pl.ds(pl.multiple_of(o * 64, 64), 64), :], sib_r.at[4])
    landed(ig_hbm.at[:, half_o], sib_r.at[5])
    landed(gg_hbm.at[:, half_o], sib_r.at[6])
    for cp in ends:
        cp.wait()
    for cp in sends:
        cp.wait_send()


def finish(
    so_in, ig_in, gg_in, pn_in, part, rows, grads, so, ig, gg, pn, wg,
    v_so, v_ig, v_gg, v_pn, v_wg, v_rows, v_grads, in_sem, out_sem,
):
    tiles = [pl.ds(t * CT, CT) for t in range(part.shape[0] // CT)]
    halves = [pl.ds(i * 4, 4) for i in range(2)]
    moves = [(part.at[t], v_wg.at[t], wg.at[t]) for t in tiles]
    plain = [(so_in, v_so, so), (ig_in, v_ig, ig), (gg_in, v_gg, gg)]
    plain += [(pn_in.at[h], v_pn.at[h], pn.at[h]) for h in halves]
    order = []
    for i in range(len(tiles)):
        order += [(i, moves[i]), (len(tiles) + i, plain[i])]

    def copy(src, dst, sem):
        cp = pltpu.make_async_copy(src, dst, sem)
        cp.start()
        return cp

    first = [copy(rows, v_rows, in_sem.at[10]), copy(grads, v_grads, in_sem.at[11])]
    loads = [copy(src, mid, in_sem.at[i]) for i, (src, mid, _) in order]
    for cp in first:
        cp.wait()
    stores = []
    for (i, (_, mid, dst)), load in zip(order, loads):
        load.wait()
        if i < len(tiles):
            mid[...] = mid[...] + lax.dot_general(
                v_rows[:, tiles[i]], v_grads[...], (((0,), (0,)), ((), ())),
                preferred_element_type=jnp.float32,
            )
        stores.append(copy(mid, dst, out_sem.at[i]))
    for cp in stores:
        cp.wait()


def local(section_inputs, output_grad, norm_gain, weight, parked, in_flight, old_hosts, new_hosts):
    rows, width = section_inputs.shape[1:]
    hc, oc = weight.shape[1:]
    f32, bf16 = jnp.float32, jnp.bfloat16
    hbm = pl.BlockSpec(memory_space=pl.ANY)
    smem = pl.BlockSpec(memory_space=pltpu.SMEM)
    vm = pltpu.VMEM
    dma = pltpu.SemaphoreType.DMA
    so_p, ig_p, wg_p, gg_p, pn_p, rows_p, grads_p = pl.pallas_call(
        kernel,
        out_shape=(
            jax.ShapeDtypeStruct((rows, width), bf16),
            jax.ShapeDtypeStruct((rows, width), bf16),
            jax.ShapeDtypeStruct((hc, oc), f32),
            jax.ShapeDtypeStruct((1, width), f32),
            jax.ShapeDtypeStruct((8, 2, 16, width), bf16),
            jax.ShapeDtypeStruct((2, 2, 64, hc), bf16),
            jax.ShapeDtypeStruct((2, 2, 64, oc), bf16),
        ),
        in_specs=[hbm] * 6 + [smem] * 3,
        out_specs=(hbm,) * 7,
        scratch_shapes=[
            vm((rows, width), bf16),
            vm((9, 16, hc), bf16),
            vm((rows, hc), bf16),
            vm((1, hc), f32),
            vm((hc, oc), bf16),
            vm((3, 8, 2, 16, hc), bf16),
            vm((8, 2, 16, hc), bf16),
            vm((16, 16, hc), bf16),
            vm((rows, hc), bf16),
            vm((rows, 128), f32),
            vm((8, 2, 16, hc), bf16),
            vm((8, 2, 16, hc), bf16),
            vm((8, 2, 64, oc), bf16),
            vm((8, 2, 64, hc), bf16),
            vm((8, 2, 64, hc), bf16),
            vm((2, 2, 64, hc), bf16),
            vm((2, 2, 64, hc), bf16),
            vm((2, 2, 64, hc), bf16),
            vm((2, 64, hc), bf16),
            vm((64, hc), bf16),
            vm((64, hc), bf16),
            vm((2, 2, 64, hc), bf16),
            vm((2, 2, 64, hc), bf16),
            vm((rows, hc), bf16),
            vm((rows, hc), bf16),
            vm((rows, hc), f32),
            vm((2, rows, 128), f32),
            vm((2, rows, 128), f32),
            vm((8, 2, 64, oc), f32),
            vm((8, 64, oc), f32),
            vm((8, 64, oc), bf16),
            vm((8, 64, oc), bf16),
            vm((64, width), bf16),
            vm((rows, hc), bf16),
            vm((hc, oc), f32),
            vm((8, 1, hc), f32),
            vm((1, hc), f32),
            dma((9,)),
            dma((8,)), dma((8,)),
            dma((8,)), dma((8,)),
            dma((8,)), dma((8,)),
            dma((9,)), dma((9,)),
            dma((12,)), dma((12,)),
            dma((10,)), dma((10,)),
            dma((7,)), dma((7,)),
            dma((11,)), dma((11,)),
            dma((8,)), dma((8,)),
            dma((7,)),
        ],
        compiler_params=pltpu.CompilerParams(
            collective_id=0, has_side_effects=True, vmem_limit_bytes=62 * 2**20
        ),
        cost_estimate=pl.CostEstimate(flops=10 * 2**30, bytes_accessed=40 * 2**20, transcendentals=0),
        name="relay_step",
    )(
        section_inputs[0], section_inputs[0].reshape(8, 16, width), output_grad[0], norm_gain, weight[0], parked[0],
        in_flight, old_hosts[0, :, 0], new_hosts[0, :, 0],
    )
    so, ig, gg, pn, wg = pl.pallas_call(
        finish,
        out_shape=(
            jax.ShapeDtypeStruct((rows, width), bf16),
            jax.ShapeDtypeStruct((rows, width), bf16),
            jax.ShapeDtypeStruct((1, width), f32),
            jax.ShapeDtypeStruct((8, 2, 16, width), bf16),
            jax.ShapeDtypeStruct((hc, oc), f32),
        ),
        in_specs=[hbm] * 7,
        out_specs=[hbm] * 5,
        scratch_shapes=[
            vm((rows, width), bf16),
            vm((rows, width), bf16),
            vm((1, width), f32),
            vm((8, 2, 16, width), bf16),
            vm((hc, oc), f32),
            vm((256, hc), bf16),
            vm((256, oc), bf16),
            dma((12,)),
            dma((10,)),
        ],
        compiler_params=pltpu.CompilerParams(vmem_limit_bytes=62 * 2**20),
        cost_estimate=pl.CostEstimate(flops=2**30, bytes_accessed=25 * 2**20, transcendentals=0),
        name="finish",
    )(so_p, ig_p, gg_p, pn_p, wg_p, rows_p.reshape(256, hc), grads_p.reshape(256, oc))
    return so[None], ig[None], wg[None], gg, pn[None]


def solution(mesh):
    in_specs = (
        P("pipe", "dp", None),
        P("pipe", "dp", None),
        P("pipe", None),
        P("pipe", "tensor", "dp"),
        P("pipe", None, None, "dp", None, None),
        P(),
        P("pipe", "dp", None),
        P("pipe", "dp", None),
    )
    out_specs = (
        P("pipe", "dp", None),
        P("pipe", "dp", None),
        P("pipe", "tensor", "dp"),
        P("pipe", None),
        P("pipe", None, "dp", None, None),
    )
    return jax.shard_map(local, mesh=mesh, in_specs=in_specs, out_specs=out_specs, check_vma=False)
```

```python
import functools

import jax
import jax.numpy as jnp
from jax import lax
from jax.experimental import pallas as pl
from jax.experimental.pallas import tpu as pltpu
from jax.sharding import PartitionSpec as P

eps = 1e-05
MESH = pl.DeviceIdType.MESH
X = 4
OWN, RIGHT, LEFT, FAR = 0, 2, 4, 6
CT = 512


def kernel(
    x_hbm, blocks_hbm, grad_hbm, gain_hbm, w_hbm, parked_hbm, flight, hosts_old, hosts_new,
    so_hbm, ig_hbm, wg_hbm, gg_hbm, pn_hbm, ago2_hbm, gc2_hbm,
    xf, xh, gh, gain, w, stage, p1s, p1r, early, oscale, p2s, p2r, gc,
    agx, ago, a2, b_r, b_l, rz2, rl2, rr2, rl1, rr1, zs, zr, sums, ng,
    part, sib_part, up, ur, us, uin, so, ig, wg, gp, gsum,
    local_sem, a2a_s, a2a_r, p1_s, p1_r, p2_s, p2_r, agx_s, agx_r, ago_s, ago_r,
    rs_s, rs_r, sib_s, sib_r, up_s, up_r, gg_s, gg_r, out_sem,
):
    f32, bf16 = jnp.float32, jnp.bfloat16
    p = lax.axis_index("pipe")
    d = lax.axis_index("dp")
    c = lax.axis_index("tensor")
    xi, zh = d // 2, lax.rem(d, 2)
    o = 1 - c
    xr, xl, x2 = lax.rem(xi + 1, X), lax.rem(xi + 3, X), lax.rem(xi + 2, X)
    dz = xi * 2 + (1 - zh)
    dr, dl = xr * 2 + zh, xl * 2 + zh
    dx2, dx2z = x2 * 2 + zh, x2 * 2 + (1 - zh)
    drz, dlz = xr * 2 + (1 - zh), xl * 2 + (1 - zh)
    hc = xh.shape[-1]
    oc = gc.shape[-1]
    right, left, zdev = (p, dr, c), (p, dl, c), (p, dz, c)
    sib = (p, d, o)
    half_c = pl.ds(pl.multiple_of(c * hc, 128), hc)

    def pipe_peer(k):
        return lax.rem(p + k, 8)

    def dp_peer(k):
        return lax.rem(d + k, 8)

    sends = []

    def remote(src, dst, ssem, rsem, dev):
        cp = pltpu.make_async_remote_copy(
            src_ref=src, dst_ref=dst, send_sem=ssem, recv_sem=rsem,
            device_id=dev, device_id_type=MESH,
        )
        cp.start()
        sends.append(cp)
        return cp

    def landed(dst, rsem):
        pltpu.make_async_copy(dst, dst, rsem).wait()

    def local(src, dst, sem):
        cp = pltpu.make_async_copy(src, dst, sem)
        cp.start()
        return cp

    c_gown = local(
        grad_hbm.at[pl.ds(c * 64, 64), pl.ds(pl.multiple_of(d * oc, 128), oc)],
        gc.at[OWN, c], local_sem.at[6],
    )
    c_xf = local(x_hbm, xf, local_sem.at[0])
    c_xh = local(blocks_hbm.at[:, :, half_c], xh.at[pl.ds(0, 8)], local_sem.at[1])
    c_gain = local(gain_hbm.at[:, half_c], gain, local_sem.at[2])
    c_stage = local(parked_hbm.at[:, :, :, :, half_c], stage, local_sem.at[3])
    c_w = local(w_hbm, w, local_sem.at[4])
    c_gh = local(grad_hbm.at[:, half_c], gh, local_sem.at[5])
    later = []

    barrier = pltpu.get_barrier_semaphore()
    for k in range(1, 8):
        pl.semaphore_signal(barrier, inc=1, device_id=(pipe_peer(k), d, c), device_id_type=MESH)
        pl.semaphore_signal(barrier, inc=1, device_id=(p, dp_peer(k), c), device_id_type=MESH)
    pl.semaphore_signal(barrier, inc=1, device_id=sib, device_id_type=MESH)
    pl.semaphore_wait(barrier, 15)

    def cols(t):
        return pl.ds(pl.multiple_of(t * CT, CT), CT)

    n_t = hc // CT

    def loop(n):
        def run(body):
            def step(i, _):
                body(i)
                return 0

            lax.fori_loop(0, n, step, 0)

        return run

    def back(rows, t):
        return lax.dot_general(
            rows, w[cols(t), :], (((1,), (1,)), ((), ())), preferred_element_type=f32
        )

    def lanes(v):
        total = v[:, 0:128]
        for i in range(1, v.shape[1] // 128):
            total = total + v[:, i * 128:(i + 1) * 128]
        return total

    def place(hosts):
        h = [hosts[b] for b in range(8)]
        return [
            h[b] * 2 + sum([jnp.where(h[a] == h[b], 1, 0) for a in range(b)], jnp.int32(0))
            for b in range(8)
        ]

    peers = [d, dz, dr, drz, dl, dlz, dx2, dx2z]
    there = [0, 1, 4, 5, 2, 3, 6, 7]

    def grads_out():
        for k in (1, 2, 4, 6, 3, 5, 7):
            q = peers[k]
            remote(
                grad_hbm.at[pl.ds(c * 64, 64), pl.ds(pl.multiple_of(q * oc, 128), oc)],
                gc.at[there[k], c], a2a_s.at[k], a2a_r.at[there[k]], (p, q, c),
            )

    def grads_sib():
        c_gown.wait()
        for k in range(1, 8):
            landed(gc.at[k, c], a2a_r.at[k])
        remote(gc.at[:, c], gc.at[:, c], sib_s.at[0], sib_r.at[0], sib)

    def grads_in():
        c_w.wait()
        landed(gc.at[:, o], sib_r.at[0])

    def norm_new():
        c_xf.wait()
        c_xh.wait()
        c_gain.wait()

        @loop(8)
        def _(i):
            rows = pl.ds(pl.multiple_of(i * 16, 16), 16)
            v = xf[rows, :].astype(f32)
            scale = lax.rsqrt(jnp.mean(v * v, axis=-1, keepdims=True) + eps)
            val = (xh[i].astype(f32) * scale * gain[...]).astype(bf16)
            agx[OWN, i // 4, pl.ds(pl.multiple_of(lax.rem(i, 4) * 16, 16), 16), :] = val

    def own_z(buf, ss, rs):
        remote(buf.at[OWN], buf.at[OWN + 1], ss.at[0], rs.at[0], zdev)

    def own_x(buf, ss, rs):
        remote(buf.at[OWN], buf.at[LEFT], ss.at[1], rs.at[1], right)
        remote(buf.at[OWN], buf.at[RIGHT], ss.at[3], rs.at[3], left)

    def z_x(buf, ss, rs):
        landed(buf.at[OWN + 1], rs.at[0])
        remote(buf.at[OWN + 1], buf.at[LEFT + 1], ss.at[2], rs.at[2], right)
        remote(buf.at[OWN + 1], buf.at[RIGHT + 1], ss.at[4], rs.at[4], left)

    def far_x(buf, ss, rs):
        landed(buf.at[LEFT], rs.at[1])
        remote(buf.at[LEFT, 0], buf.at[FAR, 0], ss.at[5], rs.at[5], right)
        landed(buf.at[RIGHT], rs.at[3])
        remote(buf.at[RIGHT, 1], buf.at[FAR, 1], ss.at[7], rs.at[7], left)

    def near_z(buf, rs):
        landed(buf.at[LEFT + 1], rs.at[2])
        landed(buf.at[RIGHT + 1], rs.at[4])

    def new_z():
        own_z(agx, agx_s, agx_r)

    def new_x():
        own_x(agx, agx_s, agx_r)

    def new_zx():
        z_x(agx, agx_s, agx_r)

    def new_far():
        far_x(agx, agx_s, agx_r)

    def new_far_z():
        for h, n in ((0, 5), (1, 7)):
            landed(agx.at[FAR, h], agx_r.at[n])
            remote(agx.at[FAR, h], agx.at[FAR + 1, h], agx_s.at[n + 1], agx_r.at[n + 1], zdev)

    def new_near():
        near_z(agx, agx_r)

    def stash_out():
        c_stage.wait()

        @loop(8)
        def _(s):
            p1s[s] = stage[jnp.maximum(flight[s] - 1, 0), s]

        for k in range(1, 8):
            q = pipe_peer(k)
            remote(p1s.at[q], p1r.at[pl.ds(p * 2, 2)], p1_s.at[k], p1_r.at[k], (q, d, c))
        later.append(local(p1s.at[p], p1r.at[pl.ds(p * 2, 2)], local_sem.at[7]))

    def norm_old():
        later.pop(0).wait()
        for k in range(1, 8):
            landed(p1r.at[pl.ds(lax.rem(p + 8 - k, 8) * 2, 2)], p1_r.at[k])
        old_at = place(hosts_old)
        for b in range(8):
            v = p1r[old_at[b]]
            early[pl.ds(b * 16, 16), :] = v
            v = v.astype(f32)
            part[0, pl.ds(b * 16, 16), :] = lanes(v * v)
        remote(part.at[0], sib_part.at[0], sib_s.at[1], sib_r.at[1], sib)
        landed(sib_part.at[0], sib_r.at[1])

        @loop(8)
        def _(i):
            rows = pl.ds(pl.multiple_of(i * 16, 16), 16)
            sq = jnp.sum(part[0, rows, :] + sib_part[0, rows, :], axis=-1, keepdims=True)
            scale = lax.rsqrt(sq / (2 * hc) + eps)
            oscale[rows, :] = jnp.broadcast_to(scale, (16, 128))
            val = (early[rows, :].astype(f32) * scale * gain[...]).astype(bf16)
            ago[OWN, i // 4, pl.ds(pl.multiple_of(lax.rem(i, 4) * 16, 16), 16), :] = val

    def old_z():
        own_z(ago, ago_s, ago_r)

    def old_x():
        own_x(ago, ago_s, ago_r)

    def old_zx():
        z_x(ago, ago_s, ago_r)

    def old_far():
        far_x(ago, ago_s, ago_r)

    def old_far_z():
        for h, n in ((0, 5), (1, 7)):
            landed(ago.at[FAR, h], ago_r.at[n])
            remote(
                ago.at[FAR, h, pl.ds(32, 32)], ago.at[FAR + 1, h, pl.ds(32, 32)],
                ago_s.at[n + 4], ago_r.at[n + 4], zdev,
            )

    def old_far_x():
        near_z(ago, ago_r)
        for h, n, at, to in ((0, 6, LEFT + 1, right), (1, 8, RIGHT + 1, left)):
            remote(
                ago.at[at, h, pl.ds(0, 32)], ago.at[FAR + 1, h, pl.ds(0, 32)],
                ago_s.at[n], ago_r.at[n], to,
            )

    def park_out():
        xh[8] = jnp.zeros((16, hc), bf16)
        new_at = place(hosts_new)
        for slot in range(16):
            which = 8 + sum([jnp.where(new_at[b] == slot, b - 8, 0) for b in range(8)], jnp.int32(0))
            p2s[slot // 2, slot % 2] = xh[which]
        for k in range(1, 8):
            q = pipe_peer(k)
            remote(p2s.at[q], p2r.at[p], p2_s.at[k], p2_r.at[k], (q, d, c))
        later.append(local(p2s.at[p], p2r.at[p], local_sem.at[8]))

    def park_sib():
        later.pop(0).wait()
        for k in range(1, 8):
            landed(p2r.at[lax.rem(p + 8 - k, 8)], p2_r.at[k])
        ends.append(local(p2r, pn_hbm.at[:, :, :, half_c], out_sem.at[6]))
        remote(p2r, pn_hbm.at[:, :, :, half_c], sib_s.at[2], sib_r.at[2], sib)

    def sum_first():
        @loop(n_t)
        def _(t):
            val = back(gc[...].reshape(1024, oc), t).reshape(8, 2, 64, CT)
            a2[1, :, :, cols(t)] = val[FAR + 1].astype(bf16)
            b_r[1, :, :, cols(t)] = val[RIGHT + 1].astype(bf16)
            b_l[1, :, :, cols(t)] = val[LEFT + 1].astype(bf16)
            b_r[0, 1, :, cols(t)] = val[RIGHT, 1].astype(bf16)
            b_l[0, 0, :, cols(t)] = val[LEFT, 0].astype(bf16)
            sums[0, :, :, cols(t)] = val[FAR]
            sums[1, 0, :, cols(t)] = val[RIGHT, 0]
            sums[1, 1, :, cols(t)] = val[LEFT, 1]
            sums[2, :, :, cols(t)] = val[OWN + 1]
            sums[3, :, :, cols(t)] = val[OWN]

        remote(a2.at[1], rz2, rs_s.at[0], rs_r.at[0], zdev)

    def sum_near_z():
        remote(b_r.at[1], rl1.at[1], rs_s.at[3], rs_r.at[3], right)
        remote(b_l.at[1], rr1.at[1], rs_s.at[4], rs_r.at[4], left)

    def sum_near():
        remote(b_r.at[0, 1], rl1.at[0, 1], rs_s.at[5], rs_r.at[5], right)
        remote(b_l.at[0, 0], rr1.at[0, 0], rs_s.at[6], rs_r.at[6], left)

    def sum_far():
        landed(rz2, rs_r.at[0])

        @loop(n_t)
        def _(t):
            a2[0, :, :, cols(t)] = (sums[0, :, :, cols(t)] + rz2[:, :, cols(t)].astype(f32)).astype(bf16)

        remote(a2.at[0, 0], rl2, rs_s.at[1], rs_r.at[1], right)
        remote(a2.at[0, 1], rr2, rs_s.at[2], rs_r.at[2], left)

    def sum_through():
        landed(rl2, rs_r.at[1])
        landed(rr2, rs_r.at[2])

        @loop(n_t)
        def _(t):
            b_r[0, 0, :, cols(t)] = (sums[1, 0, :, cols(t)] + rl2[:, cols(t)].astype(f32)).astype(bf16)
            b_l[0, 1, :, cols(t)] = (sums[1, 1, :, cols(t)] + rr2[:, cols(t)].astype(f32)).astype(bf16)

        remote(b_r.at[0, 0], rl1.at[0, 0], rs_s.at[7], rs_r.at[7], right)
        remote(b_l.at[0, 1], rr1.at[0, 1], rs_s.at[8], rs_r.at[8], left)

    def sum_z():
        landed(rl1.at[1], rs_r.at[3])
        landed(rr1.at[1], rs_r.at[4])

        @loop(n_t)
        def _(t):
            val = sums[2, :, :, cols(t)] + rl1[1, :, :, cols(t)].astype(f32)
            val = val + rr1[1, :, :, cols(t)].astype(f32)
            zs[:, cols(t)] = val.astype(bf16).reshape(128, CT)

        remote(zs, zr, rs_s.at[9], rs_r.at[9], zdev)

    def sum_own():
        landed(rl1.at[0, 1], rs_r.at[5])
        landed(rr1.at[0, 0], rs_r.at[6])
        landed(rl1.at[0, 0], rs_r.at[7])
        landed(rr1.at[0, 1], rs_r.at[8])
        landed(zr, rs_r.at[9])
        part[1] = jnp.zeros((128, 128), f32)

        @loop(n_t)
        def _(t):
            val = sums[3, :, :, cols(t)] + rl1[0, :, :, cols(t)].astype(f32)
            val = val + rr1[0, :, :, cols(t)].astype(f32)
            val = val.reshape(128, CT) + zr[:, cols(t)].astype(f32)
            ng[:, cols(t)] = val
            term = val * (early[:, cols(t)].astype(f32) * oscale[:, 0:1])
            gp[d, :, cols(t)] = jnp.sum(term, axis=0, keepdims=True)
            part[1] = part[1] + lanes(term * gain[:, cols(t)])

        remote(part.at[1], sib_part.at[1], sib_s.at[3], sib_r.at[3], sib)
        for k in range(1, 8):
            remote(gp.at[d], gp.at[d], gg_s.at[k], gg_r.at[k], (p, dp_peer(k), c))

    def project(at, i):
        two = pl.ds(at, 2)

        @loop(n_t)
        def _(t):
            val = jnp.dot(
                agx[two, :, :, cols(t)].reshape(256, CT), w[cols(t), :],
                preferred_element_type=f32,
            ).reshape(2, 2, 64, oc)

            @pl.when(t == 0)
            def _():
                up[two] = val

            @pl.when(t > 0)
            def _():
                up[two] = up[two] + val

        remote(up.at[two, o], ur.at[two], up_s.at[i], up_r.at[i], sib)

    def project_sum(at, i):
        two = pl.ds(at, 2)
        landed(ur.at[two], up_r.at[i])
        us[two] = (up[two, c] + ur[two]).astype(bf16)

    def project_own():
        project(OWN, 0)

    def project_near():
        project(RIGHT, 1)
        project(LEFT, 2)

    def project_far():
        landed(agx.at[FAR + 1, 0], agx_r.at[6])
        landed(agx.at[FAR + 1, 1], agx_r.at[8])
        project(FAR, 3)

    def update_out(ks):
        for k in ks:
            remote(us.at[k], uin.at[d], up_s.at[3 + k], up_r.at[3 + there[k]], (p, peers[k], c))

    def update_near():
        project_sum(OWN, 0)
        project_sum(RIGHT, 1)
        project_sum(LEFT, 2)
        uin[d] = us[OWN]
        update_out((1, 2, 4, 3, 5))

    def update_far():
        project_sum(FAR, 3)
        update_out((6, 7))

    mine = pl.ds(pl.multiple_of(c * 64, 64), 64)

    def output():
        for k in range(1, 8):
            landed(uin.at[peers[k]], up_r.at[3 + k])

        @loop(8)
        def _(q):
            at = pl.ds(pl.multiple_of(q * oc, 128), oc)
            so[:, at] = (xf[mine, at].astype(f32) + uin[q].astype(f32)).astype(bf16)

        ends.append(local(so, so_hbm.at[mine, :], out_sem.at[0]))
        remote(so, so_hbm.at[mine, :], sib_s.at[4], sib_r.at[4], sib)

    def input_out():
        landed(sib_part.at[1], sib_r.at[3])
        c_gh.wait()

        @loop(8)
        def _(i):
            rows = pl.ds(pl.multiple_of(i * 16, 16), 16)
            mean = jnp.sum(part[1, rows, :] + sib_part[1, rows, :], axis=-1, keepdims=True) / (2 * hc)
            scale = oscale[rows, 0:1]
            old_hat = early[rows, :].astype(f32) * scale
            centred = ng[rows, :] * gain[...] - old_hat * mean
            ig[rows, :] = (gh[rows, :].astype(f32) + scale * centred).astype(bf16)

        ends.append(local(ig, ig_hbm.at[:, half_c], out_sem.at[1]))
        remote(ig, ig_hbm.at[:, half_c], sib_s.at[5], sib_r.at[5], sib)

    def gain_out():
        for k in range(1, 8):
            landed(gp.at[0], gg_r.at[k])
        total = gp[0]
        for q in range(1, 8):
            total = total + gp[q]
        gsum[...] = total
        ends.append(local(gsum, gg_hbm.at[:, half_c], out_sem.at[2]))
        remote(gsum, gg_hbm.at[:, half_c], sib_s.at[6], sib_r.at[6], sib)

    def weight_part(at, n, first):
        some = pl.ds(at, n)

        @loop(n_t)
        def _(t):
            val = lax.dot_general(
                ago[some, :, :, cols(t)].reshape(128 * n, CT), gc[some].reshape(128 * n, oc),
                (((0,), (0,)), ((), ())), preferred_element_type=f32,
            )
            if first:
                wg[cols(t), :] = val
            else:
                wg[cols(t), :] = wg[cols(t), :] + val

    def weight_own():
        weight_part(OWN, 2, True)

    def weight_near():
        weight_part(RIGHT, 4, False)
        ends.append(local(wg, wg_hbm, out_sem.at[3]))
        ends.append(local(gc.at[pl.ds(FAR, 2)], gc2_hbm, out_sem.at[4]))

    def weight_rows():
        for n in (6, 8, 9, 11):
            landed(ago.at[FAR + 1, 0, pl.ds(0, 32)], ago_r.at[n])
        ends.append(local(ago.at[pl.ds(FAR, 2)], ago2_hbm, out_sem.at[5]))

    ends = []
    for step in (
        grads_out, norm_new, stash_out, new_z, new_x, new_far, grads_sib, grads_in,
        sum_first, sum_near, sum_near_z, new_zx, norm_old, new_far_z, sum_far, park_out,
        old_z, old_x, sum_through, old_zx, weight_own, old_far, sum_z, project_own,
        new_near, project_near, update_near, sum_own, old_far_z, project_far, input_out,
        update_far, old_far_x, park_sib, weight_near, gain_out, output, weight_rows,
    ):
        step()

    half_o = pl.ds(pl.multiple_of(o * hc, 128), hc)
    landed(pn_hbm.at[:, :, :, half_o], sib_r.at[2])
    landed(so_hbm.at[pl.ds(pl.multiple_of(o * 64, 64), 64), :], sib_r.at[4])
    landed(ig_hbm.at[:, half_o], sib_r.at[5])
    landed(gg_hbm.at[:, half_o], sib_r.at[6])
    for cp in ends:
        cp.wait()
    for cp in sends:
        cp.wait_send()


def finish(
    so_in, ig_in, gg_in, pn_in, part, rows, grads, so, ig, gg, pn, wg,
    v_so, v_ig, v_gg, v_pn, v_wg, v_rows, v_grads, in_sem, out_sem,
):
    tiles = [pl.ds(t * CT, CT) for t in range(part.shape[0] // CT)]
    halves = [pl.ds(i * 4, 4) for i in range(2)]
    moves = [(part.at[t], v_wg.at[t], wg.at[t]) for t in tiles]
    plain = [(so_in, v_so, so), (ig_in, v_ig, ig), (gg_in, v_gg, gg)]
    plain += [(pn_in.at[h], v_pn.at[h], pn.at[h]) for h in halves]
    order = []
    for i in range(len(tiles)):
        order += [(i, moves[i]), (len(tiles) + i, plain[i])]

    def copy(src, dst, sem):
        cp = pltpu.make_async_copy(src, dst, sem)
        cp.start()
        return cp

    first = [copy(rows, v_rows, in_sem.at[10]), copy(grads, v_grads, in_sem.at[11])]
    loads = [copy(src, mid, in_sem.at[i]) for i, (src, mid, _) in order]
    for cp in first:
        cp.wait()
    stores = []
    for (i, (_, mid, dst)), load in zip(order, loads):
        load.wait()
        if i < len(tiles):
            mid[...] = mid[...] + lax.dot_general(
                v_rows[:, tiles[i]], v_grads[...], (((0,), (0,)), ((), ())),
                preferred_element_type=jnp.float32,
            )
        stores.append(copy(mid, dst, out_sem.at[i]))
    for cp in stores:
        cp.wait()


def local(section_inputs, output_grad, norm_gain, weight, parked, in_flight, old_hosts, new_hosts):
    rows, width = section_inputs.shape[1:]
    hc, oc = weight.shape[1:]
    f32, bf16 = jnp.float32, jnp.bfloat16
    hbm = pl.BlockSpec(memory_space=pl.ANY)
    smem = pl.BlockSpec(memory_space=pltpu.SMEM)
    vm = pltpu.VMEM
    dma = pltpu.SemaphoreType.DMA
    so_p, ig_p, wg_p, gg_p, pn_p, rows_p, grads_p = pl.pallas_call(
        kernel,
        out_shape=(
            jax.ShapeDtypeStruct((rows, width), bf16),
            jax.ShapeDtypeStruct((rows, width), bf16),
            jax.ShapeDtypeStruct((hc, oc), f32),
            jax.ShapeDtypeStruct((1, width), f32),
            jax.ShapeDtypeStruct((8, 2, 16, width), bf16),
            jax.ShapeDtypeStruct((2, 2, 64, hc), bf16),
            jax.ShapeDtypeStruct((2, 2, 64, oc), bf16),
        ),
        in_specs=[hbm] * 6 + [smem] * 3,
        out_specs=(hbm,) * 7,
        scratch_shapes=[
            vm((rows, width), bf16),
            vm((9, 16, hc), bf16),
            vm((rows, hc), bf16),
            vm((1, hc), f32),
            vm((hc, oc), bf16),
            vm((3, 8, 2, 16, hc), bf16),
            vm((8, 2, 16, hc), bf16),
            vm((16, 16, hc), bf16),
            vm((rows, hc), bf16),
            vm((rows, 128), f32),
            vm((8, 2, 16, hc), bf16),
            vm((8, 2, 16, hc), bf16),
            vm((8, 2, 64, oc), bf16),
            vm((8, 2, 64, hc), bf16),
            vm((8, 2, 64, hc), bf16),
            vm((2, 2, 64, hc), bf16),
            vm((2, 2, 64, hc), bf16),
            vm((2, 2, 64, hc), bf16),
            vm((2, 64, hc), bf16),
            vm((64, hc), bf16),
            vm((64, hc), bf16),
            vm((2, 2, 64, hc), bf16),
            vm((2, 2, 64, hc), bf16),
            vm((rows, hc), bf16),
            vm((rows, hc), bf16),
            vm((4, 2, 64, hc), f32),
            vm((rows, hc), f32),
            vm((2, rows, 128), f32),
            vm((2, rows, 128), f32),
            vm((8, 2, 64, oc), f32),
            vm((8, 64, oc), f32),
            vm((8, 64, oc), bf16),
            vm((8, 64, oc), bf16),
            vm((64, width), bf16),
            vm((rows, hc), bf16),
            vm((hc, oc), f32),
            vm((8, 1, hc), f32),
            vm((1, hc), f32),
            dma((9,)),
            dma((8,)), dma((8,)),
            dma((8,)), dma((8,)),
            dma((8,)), dma((8,)),
            dma((9,)), dma((9,)),
            dma((12,)), dma((12,)),
            dma((10,)), dma((10,)),
            dma((7,)), dma((7,)),
            dma((11,)), dma((11,)),
            dma((8,)), dma((8,)),
            dma((7,)),
        ],
        compiler_params=pltpu.CompilerParams(
            collective_id=0, has_side_effects=True, vmem_limit_bytes=62 * 2**20
        ),
        cost_estimate=pl.CostEstimate(flops=10 * 2**30, bytes_accessed=40 * 2**20, transcendentals=0),
        name="relay_step",
    )(
        section_inputs[0], section_inputs[0].reshape(8, 16, width), output_grad[0], norm_gain, weight[0], parked[0],
        in_flight, old_hosts[0, :, 0], new_hosts[0, :, 0],
    )
    so, ig, gg, pn, wg = pl.pallas_call(
        finish,
        out_shape=(
            jax.ShapeDtypeStruct((rows, width), bf16),
            jax.ShapeDtypeStruct((rows, width), bf16),
            jax.ShapeDtypeStruct((1, width), f32),
            jax.ShapeDtypeStruct((8, 2, 16, width), bf16),
            jax.ShapeDtypeStruct((hc, oc), f32),
        ),
        in_specs=[hbm] * 7,
        out_specs=[hbm] * 5,
        scratch_shapes=[
            vm((rows, width), bf16),
            vm((rows, width), bf16),
            vm((1, width), f32),
            vm((8, 2, 16, width), bf16),
            vm((hc, oc), f32),
            vm((256, hc), bf16),
            vm((256, oc), bf16),
            dma((12,)),
            dma((10,)),
        ],
        compiler_params=pltpu.CompilerParams(vmem_limit_bytes=62 * 2**20),
        cost_estimate=pl.CostEstimate(flops=2**30, bytes_accessed=25 * 2**20, transcendentals=0),
        name="finish",
    )(so_p, ig_p, gg_p, pn_p, wg_p, rows_p.reshape(256, hc), grads_p.reshape(256, oc))
    return so[None], ig[None], wg[None], gg, pn[None]


def solution(mesh):
    in_specs = (
        P("pipe", "dp", None),
        P("pipe", "dp", None),
        P("pipe", None),
        P("pipe", "tensor", "dp"),
        P("pipe", None, None, "dp", None, None),
        P(),
        P("pipe", "dp", None),
        P("pipe", "dp", None),
    )
    out_specs = (
        P("pipe", "dp", None),
        P("pipe", "dp", None),
        P("pipe", "tensor", "dp"),
        P("pipe", None),
        P("pipe", None, "dp", None, None),
    )
    return jax.shard_map(local, mesh=mesh, in_specs=in_specs, out_specs=out_specs, check_vma=False)
```

```python
import functools

import jax
import jax.numpy as jnp
from jax import lax
from jax.experimental import pallas as pl
from jax.experimental.pallas import tpu as pltpu
from jax.sharding import PartitionSpec as P

eps = 1e-05
MESH = pl.DeviceIdType.MESH
X = 4
OWN, RIGHT, LEFT, FAR = 0, 2, 4, 6
CT = 512


def kernel(
    x_hbm, blocks_hbm, grad_hbm, gain_hbm, w_hbm, parked_hbm, flight, hosts_old, hosts_new,
    so_out, ig_out, wg_out, gg_out, pn_out, ago2_out, gc2_out,
    xf, xh, gh, gain, w, stage, p1s, p1r, early, oscale, p2s, gc,
    agx, ago, a2, b_r, b_l, rz2, rl2, rr2, rl1, rr1, zs, zr, sums, ng,
    part, sib_part, up, ur, us, uin, gp,
    local_sem, a2a_s, a2a_r, p1_s, p1_r, p2_s, p2_r, agx_s, agx_r, ago_s, ago_r,
    rs_s, rs_r, sib_s, sib_r, up_s, up_r, gg_s, gg_r, out_sem,
):
    f32, bf16 = jnp.float32, jnp.bfloat16
    p = lax.axis_index("pipe")
    d = lax.axis_index("dp")
    c = lax.axis_index("tensor")
    xi, zh = d // 2, lax.rem(d, 2)
    o = 1 - c
    xr, xl, x2 = lax.rem(xi + 1, X), lax.rem(xi + 3, X), lax.rem(xi + 2, X)
    dz = xi * 2 + (1 - zh)
    dr, dl = xr * 2 + zh, xl * 2 + zh
    dx2, dx2z = x2 * 2 + zh, x2 * 2 + (1 - zh)
    drz, dlz = xr * 2 + (1 - zh), xl * 2 + (1 - zh)
    hc = xh.shape[-1]
    oc = gc.shape[-1]
    right, left, zdev = (p, dr, c), (p, dl, c), (p, dz, c)
    sib = (p, d, o)
    half_c = pl.ds(pl.multiple_of(c * hc, 128), hc)

    def pipe_peer(k):
        return lax.rem(p + k, 8)

    def dp_peer(k):
        return lax.rem(d + k, 8)

    sends = []

    def remote(src, dst, ssem, rsem, dev):
        cp = pltpu.make_async_remote_copy(
            src_ref=src, dst_ref=dst, send_sem=ssem, recv_sem=rsem,
            device_id=dev, device_id_type=MESH,
        )
        cp.start()
        sends.append(cp)
        return cp

    def landed(dst, rsem):
        pltpu.make_async_copy(dst, dst, rsem).wait()

    def local(src, dst, sem):
        cp = pltpu.make_async_copy(src, dst, sem)
        cp.start()
        return cp

    barrier = pltpu.get_barrier_semaphore()
    for k in range(1, 8):
        pl.semaphore_signal(barrier, inc=1, device_id=(pipe_peer(k), d, c), device_id_type=MESH)
        pl.semaphore_signal(barrier, inc=1, device_id=(p, dp_peer(k), c), device_id_type=MESH)
    pl.semaphore_signal(barrier, inc=1, device_id=sib, device_id_type=MESH)

    c_gown = local(
        grad_hbm.at[pl.ds(c * 64, 64), pl.ds(pl.multiple_of(d * oc, 128), oc)],
        gc.at[OWN, c], local_sem.at[6],
    )
    c_xf = local(x_hbm, xf, local_sem.at[0])
    c_xh = local(blocks_hbm.at[:, :, half_c], xh.at[pl.ds(0, 8)], local_sem.at[1])
    c_gain = local(gain_hbm.at[:, half_c], gain, local_sem.at[2])
    later, loads = [], {}

    pl.semaphore_wait(barrier, 15)

    def cols(t):
        return pl.ds(pl.multiple_of(t * CT, CT), CT)

    n_t = hc // CT

    def loop(n):
        def run(body):
            def step(i, _):
                body(i)
                return 0

            lax.fori_loop(0, n, step, 0)

        return run

    def back(rows, t):
        return lax.dot_general(
            rows, w[cols(t), :], (((1,), (1,)), ((), ())), preferred_element_type=f32
        )

    def lanes(v):
        total = v[:, 0:128]
        for i in range(1, v.shape[1] // 128):
            total = total + v[:, i * 128:(i + 1) * 128]
        return total

    def place(hosts):
        h = [hosts[b] for b in range(8)]
        return [
            h[b] * 2 + sum([jnp.where(h[a] == h[b], 1, 0) for a in range(b)], jnp.int32(0))
            for b in range(8)
        ]

    peers = [d, dz, dr, drz, dl, dlz, dx2, dx2z]
    there = [0, 1, 4, 5, 2, 3, 6, 7]

    def grads_out():
        for k in (1, 2, 4, 6, 3, 5, 7):
            q = peers[k]
            remote(
                grad_hbm.at[pl.ds(c * 64, 64), pl.ds(pl.multiple_of(q * oc, 128), oc)],
                gc.at[there[k], c], a2a_s.at[k], a2a_r.at[there[k]], (p, q, c),
            )
        loads["stage"] = local(parked_hbm.at[:, :, :, :, half_c], stage, local_sem.at[3])

    def grads_sib():
        c_gown.wait()
        for k in range(1, 8):
            landed(gc.at[k, c], a2a_r.at[k])
        remote(gc.at[:, c], gc.at[:, c], sib_s.at[0], sib_r.at[0], sib)

    def grads_in():
        loads["w"].wait()
        loads["gh"] = local(grad_hbm.at[:, half_c], gh, local_sem.at[5])
        landed(gc.at[:, o], sib_r.at[0])

    def norm_new():
        c_xf.wait()
        c_xh.wait()
        c_gain.wait()
        loads["w"] = local(w_hbm, w, local_sem.at[4])

        @loop(8)
        def _(i):
            rows = pl.ds(pl.multiple_of(i * 16, 16), 16)
            v = xf[rows, :].astype(f32)
            scale = lax.rsqrt(jnp.mean(v * v, axis=-1, keepdims=True) + eps)
            val = (xh[i].astype(f32) * scale * gain[...]).astype(bf16)
            agx[OWN, i // 4, pl.ds(pl.multiple_of(lax.rem(i, 4) * 16, 16), 16), :] = val

    def own_z(buf, ss, rs):
        remote(buf.at[OWN], buf.at[OWN + 1], ss.at[0], rs.at[0], zdev)

    def own_x(buf, ss, rs):
        remote(buf.at[OWN], buf.at[LEFT], ss.at[1], rs.at[1], right)
        remote(buf.at[OWN], buf.at[RIGHT], ss.at[3], rs.at[3], left)

    def z_x(buf, ss, rs):
        landed(buf.at[OWN + 1], rs.at[0])
        remote(buf.at[OWN + 1], buf.at[LEFT + 1], ss.at[2], rs.at[2], right)
        remote(buf.at[OWN + 1], buf.at[RIGHT + 1], ss.at[4], rs.at[4], left)

    def far_x(buf, ss, rs):
        landed(buf.at[LEFT], rs.at[1])
        remote(buf.at[LEFT, 0], buf.at[FAR, 0], ss.at[5], rs.at[5], right)
        landed(buf.at[RIGHT], rs.at[3])
        remote(buf.at[RIGHT, 1], buf.at[FAR, 1], ss.at[7], rs.at[7], left)

    def near_z(buf, rs):
        landed(buf.at[LEFT + 1], rs.at[2])
        landed(buf.at[RIGHT + 1], rs.at[4])

    def new_z():
        own_z(agx, agx_s, agx_r)

    def new_x():
        own_x(agx, agx_s, agx_r)

    def new_zx():
        z_x(agx, agx_s, agx_r)

    def new_far():
        far_x(agx, agx_s, agx_r)

    def new_far_z():
        for h, n in ((0, 5), (1, 7)):
            landed(agx.at[FAR, h], agx_r.at[n])
            remote(agx.at[FAR, h], agx.at[FAR + 1, h], agx_s.at[n + 1], agx_r.at[n + 1], zdev)

    def new_near():
        near_z(agx, agx_r)

    def stash_out():
        loads["stage"].wait()

        @loop(8)
        def _(s):
            p1s[s] = stage[jnp.maximum(flight[s] - 1, 0), s]

        for k in range(1, 8):
            q = pipe_peer(k)
            remote(p1s.at[q], p1r.at[pl.ds(p * 2, 2)], p1_s.at[k], p1_r.at[k], (q, d, c))
        later.append(local(p1s.at[p], p1r.at[pl.ds(p * 2, 2)], local_sem.at[7]))

    def norm_old():
        later.pop(0).wait()
        for k in range(1, 8):
            landed(p1r.at[pl.ds(lax.rem(p + 8 - k, 8) * 2, 2)], p1_r.at[k])
        old_at = place(hosts_old)
        for b in range(8):
            v = p1r[old_at[b]]
            early[pl.ds(b * 16, 16), :] = v
            v = v.astype(f32)
            part[0, pl.ds(b * 16, 16), :] = lanes(v * v)
        remote(part.at[0], sib_part.at[0], sib_s.at[1], sib_r.at[1], sib)
        landed(sib_part.at[0], sib_r.at[1])

        @loop(8)
        def _(i):
            rows = pl.ds(pl.multiple_of(i * 16, 16), 16)
            sq = jnp.sum(part[0, rows, :] + sib_part[0, rows, :], axis=-1, keepdims=True)
            scale = lax.rsqrt(sq / (2 * hc) + eps)
            oscale[rows, :] = jnp.broadcast_to(scale, (16, 128))
            val = (early[rows, :].astype(f32) * scale * gain[...]).astype(bf16)
            ago[OWN, i // 4, pl.ds(pl.multiple_of(lax.rem(i, 4) * 16, 16), 16), :] = val

    def old_z():
        own_z(ago, ago_s, ago_r)

    def old_x():
        own_x(ago, ago_s, ago_r)

    def old_zx():
        z_x(ago, ago_s, ago_r)

    def old_far():
        far_x(ago, ago_s, ago_r)

    def old_far_z():
        for h, n in ((0, 5), (1, 7)):
            landed(ago.at[FAR, h], ago_r.at[n])
            remote(
                ago.at[FAR, h, pl.ds(32, 32)], ago2_out.at[1, h, pl.ds(32, 32)],
                ago_s.at[n + 4], ago_r.at[n + 4], zdev,
            )
        ends.append(local(ago.at[FAR], ago2_out.at[0], out_sem.at[1]))

    def old_far_x():
        near_z(ago, ago_r)
        for h, n, at, to in ((0, 6, LEFT + 1, right), (1, 8, RIGHT + 1, left)):
            remote(
                ago.at[at, h, pl.ds(0, 32)], ago2_out.at[1, h, pl.ds(0, 32)],
                ago_s.at[n], ago_r.at[n], to,
            )

    def park_out():
        xh[8] = jnp.zeros((16, hc), bf16)
        new_at = place(hosts_new)
        for slot in range(16):
            which = 8 + sum([jnp.where(new_at[b] == slot, b - 8, 0) for b in range(8)], jnp.int32(0))
            p2s[slot // 2, slot % 2] = xh[which]
        for k in range(1, 8):
            q = pipe_peer(k)
            remote(p2s.at[q], pn_out.at[p, :, :, half_c], p2_s.at[k], p2_r.at[k], (q, d, c))
        later.append(local(p2s.at[p], pn_out.at[p, :, :, half_c], local_sem.at[8]))

    def park_sib():
        later.pop(0).wait()
        for k in range(1, 8):
            landed(pn_out.at[lax.rem(p + 8 - k, 8), :, :, half_c], p2_r.at[k])
        remote(pn_out.at[:, :, :, half_c], pn_out.at[:, :, :, half_c], sib_s.at[2], sib_r.at[2], sib)

    def sum_first():
        @loop(n_t)
        def _(t):
            val = back(gc[...].reshape(1024, oc), t).reshape(8, 2, 64, CT)
            a2[1, :, :, cols(t)] = val[FAR + 1].astype(bf16)
            b_r[1, :, :, cols(t)] = val[RIGHT + 1].astype(bf16)
            b_l[1, :, :, cols(t)] = val[LEFT + 1].astype(bf16)
            b_r[0, 1, :, cols(t)] = val[RIGHT, 1].astype(bf16)
            b_l[0, 0, :, cols(t)] = val[LEFT, 0].astype(bf16)
            sums[0, :, :, cols(t)] = val[FAR]
            sums[1, 0, :, cols(t)] = val[RIGHT, 0]
            sums[1, 1, :, cols(t)] = val[LEFT, 1]
            sums[2, :, :, cols(t)] = val[OWN + 1]
            sums[3, :, :, cols(t)] = val[OWN]

        remote(a2.at[1], rz2, rs_s.at[0], rs_r.at[0], zdev)

    def sum_near_z():
        remote(b_r.at[1], rl1.at[1], rs_s.at[3], rs_r.at[3], right)
        remote(b_l.at[1], rr1.at[1], rs_s.at[4], rs_r.at[4], left)

    def sum_near():
        remote(b_r.at[0, 1], rl1.at[0, 1], rs_s.at[5], rs_r.at[5], right)
        remote(b_l.at[0, 0], rr1.at[0, 0], rs_s.at[6], rs_r.at[6], left)

    def sum_far():
        landed(rz2, rs_r.at[0])

        @loop(n_t)
        def _(t):
            a2[0, :, :, cols(t)] = (sums[0, :, :, cols(t)] + rz2[:, :, cols(t)].astype(f32)).astype(bf16)

        remote(a2.at[0, 0], rl2, rs_s.at[1], rs_r.at[1], right)
        remote(a2.at[0, 1], rr2, rs_s.at[2], rs_r.at[2], left)

    def sum_through():
        landed(rl2, rs_r.at[1])
        landed(rr2, rs_r.at[2])

        @loop(n_t)
        def _(t):
            b_r[0, 0, :, cols(t)] = (sums[1, 0, :, cols(t)] + rl2[:, cols(t)].astype(f32)).astype(bf16)
            b_l[0, 1, :, cols(t)] = (sums[1, 1, :, cols(t)] + rr2[:, cols(t)].astype(f32)).astype(bf16)

        remote(b_r.at[0, 0], rl1.at[0, 0], rs_s.at[7], rs_r.at[7], right)
        remote(b_l.at[0, 1], rr1.at[0, 1], rs_s.at[8], rs_r.at[8], left)

    def sum_z():
        landed(rl1.at[1], rs_r.at[3])
        landed(rr1.at[1], rs_r.at[4])

        @loop(n_t)
        def _(t):
            val = sums[2, :, :, cols(t)] + rl1[1, :, :, cols(t)].astype(f32)
            val = val + rr1[1, :, :, cols(t)].astype(f32)
            zs[:, cols(t)] = val.astype(bf16).reshape(128, CT)

        remote(zs, zr, rs_s.at[9], rs_r.at[9], zdev)

    def sum_own():
        landed(rl1.at[0, 1], rs_r.at[5])
        landed(rr1.at[0, 0], rs_r.at[6])
        landed(rl1.at[0, 0], rs_r.at[7])
        landed(rr1.at[0, 1], rs_r.at[8])
        landed(zr, rs_r.at[9])
        part[1] = jnp.zeros((128, 128), f32)

        @loop(n_t)
        def _(t):
            val = sums[3, :, :, cols(t)] + rl1[0, :, :, cols(t)].astype(f32)
            val = val + rr1[0, :, :, cols(t)].astype(f32)
            val = val.reshape(128, CT) + zr[:, cols(t)].astype(f32)
            ng[:, cols(t)] = val
            term = val * (early[:, cols(t)].astype(f32) * oscale[:, 0:1])
            gp[d, :, cols(t)] = jnp.sum(term, axis=0, keepdims=True)
            part[1] = part[1] + lanes(term * gain[:, cols(t)])

        remote(part.at[1], sib_part.at[1], sib_s.at[3], sib_r.at[3], sib)
        for k in range(1, 8):
            remote(gp.at[d], gp.at[d], gg_s.at[k], gg_r.at[k], (p, dp_peer(k), c))

    def project(at, i):
        two = pl.ds(at, 2)

        @loop(n_t)
        def _(t):
            val = jnp.dot(
                agx[two, :, :, cols(t)].reshape(256, CT), w[cols(t), :],
                preferred_element_type=f32,
            ).reshape(2, 2, 64, oc)

            @pl.when(t == 0)
            def _():
                up[two] = val

            @pl.when(t > 0)
            def _():
                up[two] = up[two] + val

        remote(up.at[two, o], ur.at[two], up_s.at[i], up_r.at[i], sib)

    def project_sum(at, i):
        two = pl.ds(at, 2)
        landed(ur.at[two], up_r.at[i])
        us[two] = (up[two, c] + ur[two]).astype(bf16)

    def project_own():
        project(OWN, 0)

    def project_near():
        project(RIGHT, 1)
        project(LEFT, 2)

    def project_far():
        landed(agx.at[FAR + 1, 0], agx_r.at[6])
        landed(agx.at[FAR + 1, 1], agx_r.at[8])
        project(FAR, 3)

    def update_out(ks):
        for k in ks:
            remote(us.at[k], uin.at[d], up_s.at[3 + k], up_r.at[3 + there[k]], (p, peers[k], c))

    def update_near():
        project_sum(OWN, 0)
        project_sum(RIGHT, 1)
        project_sum(LEFT, 2)
        uin[d] = us[OWN]
        update_out((1, 2, 4, 3, 5))

    def update_far():
        project_sum(FAR, 3)
        update_out((6, 7))

    mine = pl.ds(pl.multiple_of(c * 64, 64), 64)

    def output():
        for k in range(1, 8):
            landed(uin.at[peers[k]], up_r.at[3 + k])

        @loop(8)
        def _(q):
            at = pl.ds(pl.multiple_of(q * oc, 128), oc)
            so_out[mine, at] = (xf[mine, at].astype(f32) + uin[q].astype(f32)).astype(bf16)

        remote(so_out.at[mine, :], so_out.at[mine, :], sib_s.at[4], sib_r.at[4], sib)

    def input_out():
        landed(sib_part.at[1], sib_r.at[3])
        loads["gh"].wait()

        @loop(8)
        def _(i):
            rows = pl.ds(pl.multiple_of(i * 16, 16), 16)
            mean = jnp.sum(part[1, rows, :] + sib_part[1, rows, :], axis=-1, keepdims=True) / (2 * hc)
            scale = oscale[rows, 0:1]
            old_hat = early[rows, :].astype(f32) * scale
            centred = ng[rows, :] * gain[...] - old_hat * mean
            ig_out[rows, half_c] = (gh[rows, :].astype(f32) + scale * centred).astype(bf16)

        remote(ig_out.at[:, half_c], ig_out.at[:, half_c], sib_s.at[5], sib_r.at[5], sib)

    def gain_out():
        for k in range(1, 8):
            landed(gp.at[0], gg_r.at[k])
        total = gp[0]
        for q in range(1, 8):
            total = total + gp[q]
        gg_out[:, half_c] = total
        remote(gg_out.at[:, half_c], gg_out.at[:, half_c], sib_s.at[6], sib_r.at[6], sib)

    def weight_part(at, n, first):
        some = pl.ds(at, n)

        @loop(n_t)
        def _(t):
            val = lax.dot_general(
                ago[some, :, :, cols(t)].reshape(128 * n, CT), gc[some].reshape(128 * n, oc),
                (((0,), (0,)), ((), ())), preferred_element_type=f32,
            )
            if first:
                wg_out[cols(t), :] = val
            else:
                wg_out[cols(t), :] = wg_out[cols(t), :] + val

    def weight_own():
        weight_part(OWN, 2, True)

    def weight_near():
        weight_part(RIGHT, 4, False)
        ends.append(local(gc.at[pl.ds(FAR, 2)], gc2_out, out_sem.at[0]))

    def weight_rows():
        for n in (6, 8, 9, 11):
            landed(ago2_out.at[1, 0, pl.ds(0, 32)], ago_r.at[n])

    ends = []
    for step in (
        grads_out, norm_new, stash_out, new_x, grads_sib, grads_in, new_far, new_z,
        sum_first, sum_near_z, norm_old, old_x, new_zx, old_z, sum_far, park_out,
        sum_through, old_zx, new_far_z, sum_near, old_far, sum_z, new_near, project_own,
        project_near, update_near, project_far, old_far_z, park_sib, weight_own, sum_own,
        update_far, old_far_x, weight_near, input_out, output, weight_rows, gain_out,
    ):
        step()

    half_o = pl.ds(pl.multiple_of(o * hc, 128), hc)
    landed(pn_out.at[:, :, :, half_o], sib_r.at[2])
    landed(so_out.at[pl.ds(pl.multiple_of(o * 64, 64), 64), :], sib_r.at[4])
    landed(ig_out.at[:, half_o], sib_r.at[5])
    landed(gg_out.at[:, half_o], sib_r.at[6])
    for cp in ends:
        cp.wait()
    for cp in sends:
        cp.wait_send()


def finish(
    so_in, ig_in, gg_in, pn_in, part, rows, grads, so, ig, gg, pn, wg, v_wg, out_sem,
):
    def copy(src, dst, sem):
        cp = pltpu.make_async_copy(src, dst, sem)
        cp.start()
        return cp

    plain = [(so_in, so), (ig_in, ig), (gg_in, gg), (pn_in, pn)]
    stores = [copy(src, dst, out_sem.at[i]) for i, (src, dst) in enumerate(plain)]
    left = rows[...].reshape(256, part.shape[0])
    right = grads[...].reshape(256, part.shape[1])
    for t in range(part.shape[0] // CT):
        at = pl.ds(t * CT, CT)
        v_wg[at, :] = part[at, :] + lax.dot_general(
            left[:, t * CT:(t + 1) * CT], right, (((0,), (0,)), ((), ())),
            preferred_element_type=jnp.float32,
        )
        stores.append(copy(v_wg.at[at], wg.at[at], out_sem.at[len(plain) + t]))
    for cp in stores:
        cp.wait()


def local(section_inputs, output_grad, norm_gain, weight, parked, in_flight, old_hosts, new_hosts):
    rows, width = section_inputs.shape[1:]
    hc, oc = weight.shape[1:]
    f32, bf16 = jnp.float32, jnp.bfloat16
    hbm = pl.BlockSpec(memory_space=pl.ANY)
    smem = pl.BlockSpec(memory_space=pltpu.SMEM)
    vm = pltpu.VMEM
    vmem = pl.BlockSpec(memory_space=pltpu.VMEM)
    dma = pltpu.SemaphoreType.DMA
    so_p, ig_p, wg_p, gg_p, pn_p, rows_p, grads_p = pl.pallas_call(
        kernel,
        out_shape=(
            vm((rows, width), bf16),
            vm((rows, width), bf16),
            vm((hc, oc), f32),
            vm((1, width), f32),
            vm((8, 2, 16, width), bf16),
            vm((2, 2, 64, hc), bf16),
            vm((2, 2, 64, oc), bf16),
        ),
        in_specs=[hbm] * 6 + [smem] * 3,
        out_specs=(vmem,) * 7,
        scratch_shapes=[
            vm((rows, width), bf16),
            vm((9, 16, hc), bf16),
            vm((rows, hc), bf16),
            vm((1, hc), f32),
            vm((hc, oc), bf16),
            vm((3, 8, 2, 16, hc), bf16),
            vm((8, 2, 16, hc), bf16),
            vm((16, 16, hc), bf16),
            vm((rows, hc), bf16),
            vm((rows, 128), f32),
            vm((8, 2, 16, hc), bf16),
            vm((8, 2, 64, oc), bf16),
            vm((8, 2, 64, hc), bf16),
            vm((8, 2, 64, hc), bf16),
            vm((2, 2, 64, hc), bf16),
            vm((2, 2, 64, hc), bf16),
            vm((2, 2, 64, hc), bf16),
            vm((2, 64, hc), bf16),
            vm((64, hc), bf16),
            vm((64, hc), bf16),
            vm((2, 2, 64, hc), bf16),
            vm((2, 2, 64, hc), bf16),
            vm((rows, hc), bf16),
            vm((rows, hc), bf16),
            vm((4, 2, 64, hc), f32),
            vm((rows, hc), f32),
            vm((2, rows, 128), f32),
            vm((2, rows, 128), f32),
            vm((8, 2, 64, oc), f32),
            vm((8, 64, oc), f32),
            vm((8, 64, oc), bf16),
            vm((8, 64, oc), bf16),
            vm((8, 1, hc), f32),
            dma((9,)),
            dma((8,)), dma((8,)),
            dma((8,)), dma((8,)),
            dma((8,)), dma((8,)),
            dma((9,)), dma((9,)),
            dma((12,)), dma((12,)),
            dma((10,)), dma((10,)),
            dma((7,)), dma((7,)),
            dma((11,)), dma((11,)),
            dma((8,)), dma((8,)),
            dma((2,)),
        ],
        compiler_params=pltpu.CompilerParams(
            collective_id=0, has_side_effects=True, vmem_limit_bytes=51 * 2**20
        ),
        cost_estimate=pl.CostEstimate(flops=10 * 2**30, bytes_accessed=40 * 2**20, transcendentals=0),
        name="relay_step",
    )(
        section_inputs[0], section_inputs[0].reshape(8, 16, width), output_grad[0], norm_gain, weight[0], parked[0],
        in_flight, old_hosts[0, :, 0], new_hosts[0, :, 0],
    )
    so, ig, gg, pn, wg = pl.pallas_call(
        finish,
        out_shape=(
            jax.ShapeDtypeStruct((rows, width), bf16),
            jax.ShapeDtypeStruct((rows, width), bf16),
            jax.ShapeDtypeStruct((1, width), f32),
            jax.ShapeDtypeStruct((8, 2, 16, width), bf16),
            jax.ShapeDtypeStruct((hc, oc), f32),
        ),
        in_specs=[vmem] * 7,
        out_specs=[hbm] * 5,
        scratch_shapes=[vm((hc, oc), f32), dma((9,))],
        compiler_params=pltpu.CompilerParams(vmem_limit_bytes=32 * 2**20),
        cost_estimate=pl.CostEstimate(flops=2**30, bytes_accessed=12 * 2**20, transcendentals=0),
        name="finish",
    )(so_p, ig_p, gg_p, pn_p, wg_p, rows_p, grads_p)
    return so[None], ig[None], wg[None], gg, pn[None]


def solution(mesh):
    in_specs = (
        P("pipe", "dp", None),
        P("pipe", "dp", None),
        P("pipe", None),
        P("pipe", "tensor", "dp"),
        P("pipe", None, None, "dp", None, None),
        P(),
        P("pipe", "dp", None),
        P("pipe", "dp", None),
    )
    out_specs = (
        P("pipe", "dp", None),
        P("pipe", "dp", None),
        P("pipe", "tensor", "dp"),
        P("pipe", None),
        P("pipe", None, "dp", None, None),
    )
    return jax.shard_map(local, mesh=mesh, in_specs=in_specs, out_specs=out_specs, check_vma=False)
```

```python
import functools

import jax
import jax.numpy as jnp
from jax import lax
from jax.experimental import pallas as pl
from jax.experimental.pallas import tpu as pltpu
from jax.sharding import PartitionSpec as P

eps = 1e-05
MESH = pl.DeviceIdType.MESH
X = 4
OWN, RIGHT, LEFT, FAR = 0, 2, 4, 6
CT = 512


def kernel(
    x_hbm, blocks_hbm, grad_hbm, gain_hbm, w_hbm, parked_hbm, flight, hosts_old, hosts_new,
    so_out, ig_out, wg_out, gg_out, pn_out, ago2_out, gc2_out,
    xf, xh, gh, gain, w, stage, p1s, p1r, early, oscale, p2s, gc,
    agx, ago, a2, b_r, b_l, rz2, rl2, rr2, rl1, rr1, zs, zr, sums, ng,
    part, sib_part, up, ur, us, uin, gp,
    local_sem, a2a_s, a2a_r, p1_s, p1_r, p2_s, p2_r, agx_s, agx_r, ago_s, ago_r,
    rs_s, rs_r, sib_s, sib_r, up_s, up_r, gg_s, gg_r, out_sem,
):
    f32, bf16 = jnp.float32, jnp.bfloat16
    p = lax.axis_index("pipe")
    d = lax.axis_index("dp")
    c = lax.axis_index("tensor")
    xi, zh = d // 2, lax.rem(d, 2)
    o = 1 - c
    xr, xl, x2 = lax.rem(xi + 1, X), lax.rem(xi + 3, X), lax.rem(xi + 2, X)
    dz = xi * 2 + (1 - zh)
    dr, dl = xr * 2 + zh, xl * 2 + zh
    dx2, dx2z = x2 * 2 + zh, x2 * 2 + (1 - zh)
    drz, dlz = xr * 2 + (1 - zh), xl * 2 + (1 - zh)
    hc = xh.shape[-1]
    oc = gc.shape[-1]
    right, left, zdev = (p, dr, c), (p, dl, c), (p, dz, c)
    sib = (p, d, o)
    half_c = pl.ds(pl.multiple_of(c * hc, 128), hc)

    def pipe_peer(k):
        return lax.rem(p + k, 8)

    def dp_peer(k):
        return lax.rem(d + k, 8)

    sends = []

    def remote(src, dst, ssem, rsem, dev):
        cp = pltpu.make_async_remote_copy(
            src_ref=src, dst_ref=dst, send_sem=ssem, recv_sem=rsem,
            device_id=dev, device_id_type=MESH,
        )
        cp.start()
        sends.append(cp)
        return cp

    def landed(dst, rsem):
        pltpu.make_async_copy(dst, dst, rsem).wait()

    def local(src, dst, sem):
        cp = pltpu.make_async_copy(src, dst, sem)
        cp.start()
        return cp

    barrier = pltpu.get_barrier_semaphore()
    for k in range(1, 8):
        pl.semaphore_signal(barrier, inc=1, device_id=(pipe_peer(k), d, c), device_id_type=MESH)
        pl.semaphore_signal(barrier, inc=1, device_id=(p, dp_peer(k), c), device_id_type=MESH)
    pl.semaphore_signal(barrier, inc=1, device_id=sib, device_id_type=MESH)

    c_gown = local(
        grad_hbm.at[pl.ds(c * 64, 64), pl.ds(pl.multiple_of(d * oc, 128), oc)],
        gc.at[OWN, c], local_sem.at[6],
    )
    c_xf = local(x_hbm, xf, local_sem.at[0])
    c_xh = local(blocks_hbm.at[:, :, half_c], xh.at[pl.ds(0, 8)], local_sem.at[1])
    c_gain = local(gain_hbm.at[:, half_c], gain, local_sem.at[2])
    later, loads = [], {}

    pl.semaphore_wait(barrier, 15)

    def cols(t):
        return pl.ds(pl.multiple_of(t * CT, CT), CT)

    n_t = hc // CT

    def loop(n):
        def run(body):
            def step(i, _):
                body(i)
                return 0

            lax.fori_loop(0, n, step, 0)

        return run

    def back(rows, t):
        return lax.dot_general(
            rows, w[cols(t), :], (((1,), (1,)), ((), ())), preferred_element_type=f32
        )

    def lanes(v):
        total = v[:, 0:128]
        for i in range(1, v.shape[1] // 128):
            total = total + v[:, i * 128:(i + 1) * 128]
        return total

    def place(hosts):
        h = [hosts[b] for b in range(8)]
        return [
            h[b] * 2 + sum([jnp.where(h[a] == h[b], 1, 0) for a in range(b)], jnp.int32(0))
            for b in range(8)
        ]

    peers = [d, dz, dr, drz, dl, dlz, dx2, dx2z]
    there = [0, 1, 4, 5, 2, 3, 6, 7]

    def grads_out():
        for k in (1, 2, 4, 6, 3, 5, 7):
            q = peers[k]
            remote(
                grad_hbm.at[pl.ds(c * 64, 64), pl.ds(pl.multiple_of(q * oc, 128), oc)],
                gc.at[there[k], c], a2a_s.at[k], a2a_r.at[there[k]], (p, q, c),
            )
        loads["stage"] = local(parked_hbm.at[:, :, :, :, half_c], stage, local_sem.at[3])

    def grads_sib():
        c_gown.wait()
        for k in range(1, 8):
            landed(gc.at[k, c], a2a_r.at[k])
        remote(gc.at[:, c], gc.at[:, c], sib_s.at[0], sib_r.at[0], sib)

    def grads_in():
        loads["w"].wait()
        loads["gh"] = local(grad_hbm.at[:, half_c], gh, local_sem.at[5])
        landed(gc.at[:, o], sib_r.at[0])

    def norm_new():
        c_xf.wait()
        c_xh.wait()
        c_gain.wait()
        loads["w"] = local(w_hbm, w, local_sem.at[4])

        @loop(8)
        def _(i):
            rows = pl.ds(pl.multiple_of(i * 16, 16), 16)
            v = xf[rows, :].astype(f32)
            scale = lax.rsqrt(jnp.mean(v * v, axis=-1, keepdims=True) + eps)
            val = (xh[i].astype(f32) * scale * gain[...]).astype(bf16)
            agx[OWN, i // 4, pl.ds(pl.multiple_of(lax.rem(i, 4) * 16, 16), 16), :] = val

    def own_z(buf, ss, rs):
        remote(buf.at[OWN], buf.at[OWN + 1], ss.at[0], rs.at[0], zdev)

    def own_x(buf, ss, rs):
        remote(buf.at[OWN], buf.at[LEFT], ss.at[1], rs.at[1], right)
        remote(buf.at[OWN], buf.at[RIGHT], ss.at[3], rs.at[3], left)

    def z_x(buf, ss, rs):
        landed(buf.at[OWN + 1], rs.at[0])
        remote(buf.at[OWN + 1], buf.at[LEFT + 1], ss.at[2], rs.at[2], right)
        remote(buf.at[OWN + 1], buf.at[RIGHT + 1], ss.at[4], rs.at[4], left)

    def far_x(buf, ss, rs):
        landed(buf.at[LEFT], rs.at[1])
        remote(buf.at[LEFT, 0], buf.at[FAR, 0], ss.at[5], rs.at[5], right)
        landed(buf.at[RIGHT], rs.at[3])
        remote(buf.at[RIGHT, 1], buf.at[FAR, 1], ss.at[7], rs.at[7], left)

    def near_z(buf, rs):
        landed(buf.at[LEFT + 1], rs.at[2])
        landed(buf.at[RIGHT + 1], rs.at[4])

    def new_z():
        own_z(agx, agx_s, agx_r)

    def new_x():
        own_x(agx, agx_s, agx_r)

    def new_zx():
        z_x(agx, agx_s, agx_r)

    def new_far():
        far_x(agx, agx_s, agx_r)

    def new_far_z():
        for h, n in ((0, 5), (1, 7)):
            landed(agx.at[FAR, h], agx_r.at[n])
            remote(agx.at[FAR, h], agx.at[FAR + 1, h], agx_s.at[n + 1], agx_r.at[n + 1], zdev)

    def new_near():
        near_z(agx, agx_r)

    def stash_out():
        loads["stage"].wait()

        @loop(8)
        def _(s):
            p1s[s] = stage[jnp.maximum(flight[s] - 1, 0), s]

        for k in range(1, 8):
            q = pipe_peer(k)
            remote(p1s.at[q], p1r.at[pl.ds(p * 2, 2)], p1_s.at[k], p1_r.at[k], (q, d, c))
        later.append(local(p1s.at[p], p1r.at[pl.ds(p * 2, 2)], local_sem.at[7]))

    def norm_old():
        later.pop(0).wait()
        for k in range(1, 8):
            landed(p1r.at[pl.ds(lax.rem(p + 8 - k, 8) * 2, 2)], p1_r.at[k])
        old_at = place(hosts_old)
        for b in range(8):
            v = p1r[old_at[b]]
            early[pl.ds(b * 16, 16), :] = v
            v = v.astype(f32)
            part[0, pl.ds(b * 16, 16), :] = lanes(v * v)
        remote(part.at[0], sib_part.at[0], sib_s.at[1], sib_r.at[1], sib)
        landed(sib_part.at[0], sib_r.at[1])

        @loop(8)
        def _(i):
            rows = pl.ds(pl.multiple_of(i * 16, 16), 16)
            sq = jnp.sum(part[0, rows, :] + sib_part[0, rows, :], axis=-1, keepdims=True)
            scale = lax.rsqrt(sq / (2 * hc) + eps)
            oscale[rows, :] = jnp.broadcast_to(scale, (16, 128))
            val = (early[rows, :].astype(f32) * scale * gain[...]).astype(bf16)
            ago[OWN, i // 4, pl.ds(pl.multiple_of(lax.rem(i, 4) * 16, 16), 16), :] = val

    def old_z():
        own_z(ago, ago_s, ago_r)

    def old_x():
        own_x(ago, ago_s, ago_r)

    def old_zx():
        z_x(ago, ago_s, ago_r)

    def old_far():
        far_x(ago, ago_s, ago_r)

    def old_far_z():
        for h, n in ((0, 5), (1, 7)):
            landed(ago.at[FAR, h], ago_r.at[n])
            remote(
                ago.at[FAR, h, pl.ds(48, 16)], ago2_out.at[1, h, pl.ds(48, 16)],
                ago_s.at[n + 4], ago_r.at[n + 4], zdev,
            )
        ends.append(local(ago.at[FAR], ago2_out.at[0], out_sem.at[1]))

    def old_far_x():
        near_z(ago, ago_r)
        for h, n, at, to in ((0, 6, LEFT + 1, right), (1, 8, RIGHT + 1, left)):
            remote(
                ago.at[at, h, pl.ds(0, 48)], ago2_out.at[1, h, pl.ds(0, 48)],
                ago_s.at[n], ago_r.at[n], to,
            )

    def park_out():
        xh[8] = jnp.zeros((16, hc), bf16)
        new_at = place(hosts_new)
        for slot in range(16):
            which = 8 + sum([jnp.where(new_at[b] == slot, b - 8, 0) for b in range(8)], jnp.int32(0))
            p2s[slot // 2, slot % 2] = xh[which]
        for k in range(1, 8):
            q = pipe_peer(k)
            remote(p2s.at[q], pn_out.at[p, :, :, half_c], p2_s.at[k], p2_r.at[k], (q, d, c))
        later.append(local(p2s.at[p], pn_out.at[p, :, :, half_c], local_sem.at[8]))

    def park_sib():
        later.pop(0).wait()
        for k in range(1, 8):
            landed(pn_out.at[lax.rem(p + 8 - k, 8), :, :, half_c], p2_r.at[k])
        remote(pn_out.at[:, :, :, half_c], pn_out.at[:, :, :, half_c], sib_s.at[2], sib_r.at[2], sib)

    def sum_first():
        @loop(n_t)
        def _(t):
            val = back(gc[...].reshape(1024, oc), t).reshape(8, 2, 64, CT)
            a2[1, :, :, cols(t)] = val[FAR + 1].astype(bf16)
            b_r[1, :, :, cols(t)] = val[RIGHT + 1].astype(bf16)
            b_l[1, :, :, cols(t)] = val[LEFT + 1].astype(bf16)
            b_r[0, 1, :, cols(t)] = val[RIGHT, 1].astype(bf16)
            b_l[0, 0, :, cols(t)] = val[LEFT, 0].astype(bf16)
            sums[0, :, :, cols(t)] = val[FAR]
            sums[1, 0, :, cols(t)] = val[RIGHT, 0]
            sums[1, 1, :, cols(t)] = val[LEFT, 1]
            sums[2, :, :, cols(t)] = val[OWN + 1]
            sums[3, :, :, cols(t)] = val[OWN]

        remote(a2.at[1], rz2, rs_s.at[0], rs_r.at[0], zdev)

    def sum_near_z():
        remote(b_r.at[1], rl1.at[1], rs_s.at[3], rs_r.at[3], right)
        remote(b_l.at[1], rr1.at[1], rs_s.at[4], rs_r.at[4], left)

    def sum_near():
        remote(b_r.at[0, 1], rl1.at[0, 1], rs_s.at[5], rs_r.at[5], right)
        remote(b_l.at[0, 0], rr1.at[0, 0], rs_s.at[6], rs_r.at[6], left)

    def sum_far():
        landed(rz2, rs_r.at[0])

        @loop(n_t)
        def _(t):
            a2[0, :, :, cols(t)] = (sums[0, :, :, cols(t)] + rz2[:, :, cols(t)].astype(f32)).astype(bf16)

        remote(a2.at[0, 0], rl2, rs_s.at[1], rs_r.at[1], right)
        remote(a2.at[0, 1], rr2, rs_s.at[2], rs_r.at[2], left)

    def sum_through():
        landed(rl2, rs_r.at[1])
        landed(rr2, rs_r.at[2])

        @loop(n_t)
        def _(t):
            b_r[0, 0, :, cols(t)] = (sums[1, 0, :, cols(t)] + rl2[:, cols(t)].astype(f32)).astype(bf16)
            b_l[0, 1, :, cols(t)] = (sums[1, 1, :, cols(t)] + rr2[:, cols(t)].astype(f32)).astype(bf16)

        remote(b_r.at[0, 0], rl1.at[0, 0], rs_s.at[7], rs_r.at[7], right)
        remote(b_l.at[0, 1], rr1.at[0, 1], rs_s.at[8], rs_r.at[8], left)

    def sum_z():
        landed(rl1.at[1], rs_r.at[3])
        landed(rr1.at[1], rs_r.at[4])

        @loop(n_t)
        def _(t):
            val = sums[2, :, :, cols(t)] + rl1[1, :, :, cols(t)].astype(f32)
            val = val + rr1[1, :, :, cols(t)].astype(f32)
            zs[:, cols(t)] = val.astype(bf16).reshape(128, CT)

        remote(zs, zr, rs_s.at[9], rs_r.at[9], zdev)

    def sum_own():
        landed(rl1.at[0, 1], rs_r.at[5])
        landed(rr1.at[0, 0], rs_r.at[6])
        landed(rl1.at[0, 0], rs_r.at[7])
        landed(rr1.at[0, 1], rs_r.at[8])
        landed(zr, rs_r.at[9])
        part[1] = jnp.zeros((128, 128), f32)

        @loop(n_t)
        def _(t):
            val = sums[3, :, :, cols(t)] + rl1[0, :, :, cols(t)].astype(f32)
            val = val + rr1[0, :, :, cols(t)].astype(f32)
            val = val.reshape(128, CT) + zr[:, cols(t)].astype(f32)
            ng[:, cols(t)] = val
            term = val * (early[:, cols(t)].astype(f32) * oscale[:, 0:1])
            gp[d, :, cols(t)] = jnp.sum(term, axis=0, keepdims=True)
            part[1] = part[1] + lanes(term * gain[:, cols(t)])

        remote(part.at[1], sib_part.at[1], sib_s.at[3], sib_r.at[3], sib)
        for k in range(1, 8):
            remote(gp.at[d], gp.at[d], gg_s.at[k], gg_r.at[k], (p, dp_peer(k), c))

    def project(at, n, i):
        some = pl.ds(at, n)

        @loop(2)
        def _(t):
            half = pl.ds(pl.multiple_of(t * (hc // 2), 128), hc // 2)
            val = jnp.dot(
                agx[some, :, :, half].reshape(128 * n, hc // 2), w[half, :],
                preferred_element_type=f32,
            ).reshape(n, 2, 64, oc)

            @pl.when(t == 0)
            def _():
                up[some] = val

            @pl.when(t > 0)
            def _():
                up[some] = up[some] + val

        remote(up.at[some, o], ur.at[some], up_s.at[i], up_r.at[i], sib)

    def project_sum(at, n, i):
        some = pl.ds(at, n)
        landed(ur.at[some], up_r.at[i])
        us[some] = (up[some, c] + ur[some]).astype(bf16)

    def project_own():
        project(OWN, 2, 0)

    def project_near():
        project(RIGHT, 4, 1)

    def project_far():
        landed(agx.at[FAR + 1, 0], agx_r.at[6])
        landed(agx.at[FAR + 1, 1], agx_r.at[8])
        project(FAR, 2, 3)

    def update_out(ks):
        for k in ks:
            remote(us.at[k], uin.at[d], up_s.at[3 + k], up_r.at[3 + there[k]], (p, peers[k], c))

    def update_near():
        project_sum(OWN, 2, 0)
        project_sum(RIGHT, 4, 1)
        uin[d] = us[OWN]
        update_out((1, 2, 4, 3, 5))

    def update_far():
        project_sum(FAR, 2, 3)
        update_out((6, 7))

    mine = pl.ds(pl.multiple_of(c * 64, 64), 64)

    def output():
        for k in range(1, 8):
            landed(uin.at[peers[k]], up_r.at[3 + k])

        @loop(8)
        def _(q):
            at = pl.ds(pl.multiple_of(q * oc, 128), oc)
            so_out[mine, at] = (xf[mine, at].astype(f32) + uin[q].astype(f32)).astype(bf16)

        remote(so_out.at[mine, :], so_out.at[mine, :], sib_s.at[4], sib_r.at[4], sib)

    def input_out():
        landed(sib_part.at[1], sib_r.at[3])
        loads["gh"].wait()

        @loop(8)
        def _(i):
            rows = pl.ds(pl.multiple_of(i * 16, 16), 16)
            mean = jnp.sum(part[1, rows, :] + sib_part[1, rows, :], axis=-1, keepdims=True) / (2 * hc)
            scale = oscale[rows, 0:1]
            old_hat = early[rows, :].astype(f32) * scale
            centred = ng[rows, :] * gain[...] - old_hat * mean
            ig_out[rows, half_c] = (gh[rows, :].astype(f32) + scale * centred).astype(bf16)

        remote(ig_out.at[:, half_c], ig_out.at[:, half_c], sib_s.at[5], sib_r.at[5], sib)

    def gain_out():
        for k in range(1, 8):
            landed(gp.at[0], gg_r.at[k])
        total = gp[0]
        for q in range(1, 8):
            total = total + gp[q]
        gg_out[:, half_c] = total
        remote(gg_out.at[:, half_c], gg_out.at[:, half_c], sib_s.at[6], sib_r.at[6], sib)

    def weight_part(at, n, first):
        some = pl.ds(at, n)

        @loop(n_t)
        def _(t):
            val = lax.dot_general(
                ago[some, :, :, cols(t)].reshape(128 * n, CT), gc[some].reshape(128 * n, oc),
                (((0,), (0,)), ((), ())), preferred_element_type=f32,
            )
            if first:
                wg_out[cols(t), :] = val
            else:
                wg_out[cols(t), :] = wg_out[cols(t), :] + val

    def weight_own():
        weight_part(OWN, 2, True)

    def weight_near():
        weight_part(RIGHT, 4, False)
        ends.append(local(gc.at[pl.ds(FAR, 2)], gc2_out, out_sem.at[0]))

    def weight_rows():
        for n in (6, 8):
            landed(ago2_out.at[1, 0, pl.ds(0, 48)], ago_r.at[n])
        for n in (9, 11):
            landed(ago2_out.at[1, 0, pl.ds(48, 16)], ago_r.at[n])

    ends = []
    for step in (
        grads_out, norm_new, stash_out, new_x, grads_sib, grads_in, sum_first, new_far,
        sum_near_z, new_z, norm_old, old_x, sum_far, new_zx, old_z, park_out, sum_through,
        old_zx, new_far_z, sum_near, old_far, sum_z, new_near, project_own, project_near,
        update_near, project_far, old_far_z, park_sib, weight_own, sum_own, update_far,
        old_far_x, weight_near, input_out, gain_out, output, weight_rows,
    ):
        step()

    half_o = pl.ds(pl.multiple_of(o * hc, 128), hc)
    landed(pn_out.at[:, :, :, half_o], sib_r.at[2])
    landed(so_out.at[pl.ds(pl.multiple_of(o * 64, 64), 64), :], sib_r.at[4])
    landed(ig_out.at[:, half_o], sib_r.at[5])
    landed(gg_out.at[:, half_o], sib_r.at[6])
    for cp in ends:
        cp.wait()
    for cp in sends:
        cp.wait_send()


def finish(
    so_in, ig_in, gg_in, pn_in, part, rows, grads, so, ig, gg, pn, wg, v_wg, out_sem,
):
    def copy(src, dst, sem):
        cp = pltpu.make_async_copy(src, dst, sem)
        cp.start()
        return cp

    plain = [(so_in, so), (ig_in, ig), (gg_in, gg), (pn_in, pn)]
    stores = [copy(src, dst, out_sem.at[i]) for i, (src, dst) in enumerate(plain)]
    left = rows[...].reshape(256, part.shape[0])
    right = grads[...].reshape(256, part.shape[1])
    for t in range(part.shape[0] // CT):
        at = pl.ds(t * CT, CT)
        v_wg[at, :] = part[at, :] + lax.dot_general(
            left[:, t * CT:(t + 1) * CT], right, (((0,), (0,)), ((), ())),
            preferred_element_type=jnp.float32,
        )
        stores.append(copy(v_wg.at[at], wg.at[at], out_sem.at[len(plain) + t]))
    for cp in stores:
        cp.wait()


def local(section_inputs, output_grad, norm_gain, weight, parked, in_flight, old_hosts, new_hosts):
    rows, width = section_inputs.shape[1:]
    hc, oc = weight.shape[1:]
    f32, bf16 = jnp.float32, jnp.bfloat16
    hbm = pl.BlockSpec(memory_space=pl.ANY)
    smem = pl.BlockSpec(memory_space=pltpu.SMEM)
    vm = pltpu.VMEM
    vmem = pl.BlockSpec(memory_space=pltpu.VMEM)
    dma = pltpu.SemaphoreType.DMA
    so_p, ig_p, wg_p, gg_p, pn_p, rows_p, grads_p = pl.pallas_call(
        kernel,
        out_shape=(
            vm((rows, width), bf16),
            vm((rows, width), bf16),
            vm((hc, oc), f32),
            vm((1, width), f32),
            vm((8, 2, 16, width), bf16),
            vm((2, 2, 64, hc), bf16),
            vm((2, 2, 64, oc), bf16),
        ),
        in_specs=[hbm] * 6 + [smem] * 3,
        out_specs=(vmem,) * 7,
        scratch_shapes=[
            vm((rows, width), bf16),
            vm((9, 16, hc), bf16),
            vm((rows, hc), bf16),
            vm((1, hc), f32),
            vm((hc, oc), bf16),
            vm((3, 8, 2, 16, hc), bf16),
            vm((8, 2, 16, hc), bf16),
            vm((16, 16, hc), bf16),
            vm((rows, hc), bf16),
            vm((rows, 128), f32),
            vm((8, 2, 16, hc), bf16),
            vm((8, 2, 64, oc), bf16),
            vm((8, 2, 64, hc), bf16),
            vm((8, 2, 64, hc), bf16),
            vm((2, 2, 64, hc), bf16),
            vm((2, 2, 64, hc), bf16),
            vm((2, 2, 64, hc), bf16),
            vm((2, 64, hc), bf16),
            vm((64, hc), bf16),
            vm((64, hc), bf16),
            vm((2, 2, 64, hc), bf16),
            vm((2, 2, 64, hc), bf16),
            vm((rows, hc), bf16),
            vm((rows, hc), bf16),
            vm((4, 2, 64, hc), f32),
            vm((rows, hc), f32),
            vm((2, rows, 128), f32),
            vm((2, rows, 128), f32),
            vm((8, 2, 64, oc), f32),
            vm((8, 64, oc), f32),
            vm((8, 64, oc), bf16),
            vm((8, 64, oc), bf16),
            vm((8, 1, hc), f32),
            dma((9,)),
            dma((8,)), dma((8,)),
            dma((8,)), dma((8,)),
            dma((8,)), dma((8,)),
            dma((9,)), dma((9,)),
            dma((12,)), dma((12,)),
            dma((10,)), dma((10,)),
            dma((7,)), dma((7,)),
            dma((11,)), dma((11,)),
            dma((8,)), dma((8,)),
            dma((2,)),
        ],
        compiler_params=pltpu.CompilerParams(
            collective_id=0, has_side_effects=True, vmem_limit_bytes=51 * 2**20
        ),
        cost_estimate=pl.CostEstimate(flops=10 * 2**30, bytes_accessed=40 * 2**20, transcendentals=0),
        name="relay_step",
    )(
        section_inputs[0], section_inputs[0].reshape(8, 16, width), output_grad[0], norm_gain, weight[0], parked[0],
        in_flight, old_hosts[0, :, 0], new_hosts[0, :, 0],
    )
    so, ig, gg, pn, wg = pl.pallas_call(
        finish,
        out_shape=(
            jax.ShapeDtypeStruct((rows, width), bf16),
            jax.ShapeDtypeStruct((rows, width), bf16),
            jax.ShapeDtypeStruct((1, width), f32),
            jax.ShapeDtypeStruct((8, 2, 16, width), bf16),
            jax.ShapeDtypeStruct((hc, oc), f32),
        ),
        in_specs=[vmem] * 7,
        out_specs=[hbm] * 5,
        scratch_shapes=[vm((hc, oc), f32), dma((9,))],
        compiler_params=pltpu.CompilerParams(vmem_limit_bytes=32 * 2**20),
        cost_estimate=pl.CostEstimate(flops=2**30, bytes_accessed=12 * 2**20, transcendentals=0),
        name="finish",
    )(so_p, ig_p, gg_p, pn_p, wg_p, rows_p, grads_p)
    return so[None], ig[None], wg[None], gg, pn[None]


def solution(mesh):
    in_specs = (
        P("pipe", "dp", None),
        P("pipe", "dp", None),
        P("pipe", None),
        P("pipe", "tensor", "dp"),
        P("pipe", None, None, "dp", None, None),
        P(),
        P("pipe", "dp", None),
        P("pipe", "dp", None),
    )
    out_specs = (
        P("pipe", "dp", None),
        P("pipe", "dp", None),
        P("pipe", "tensor", "dp"),
        P("pipe", None),
        P("pipe", None, "dp", None, None),
    )
    return jax.shard_map(local, mesh=mesh, in_specs=in_specs, out_specs=out_specs, check_vma=False)
```
